512 devices in a mesh: beam: 64 (over x, z, core), head: 8 (over y).
Axes of the slice: x: 4, y: 8, z: 8, core: 2. Of those that a mesh axis runs over, the one named last changes fastest.
Arguments:
- queries: bfloat16 [256, 8192], P('beam', 'head')
- new_keys: bfloat16 [256, 1024], P('beam', 'head')
- new_values: bfloat16 [256, 1024], P('beam', 'head'), may hold values from -6 to 6
- prompt_keys: bfloat16 [16, 16384, 1024], P(None, 'beam', 'head')
- prompt_values: bfloat16 [16, 16384, 1024], P(None, 'beam', 'head'), may hold values from -6 to 6
- private_keys: bfloat16 [256, 512, 1024], P('beam', None, 'head'), may hold values from -16 to 16
- private_values: bfloat16 [256, 512, 1024], P('beam', None, 'head'), may hold values from -6 to 6
- parents: int32 [256], P('beam'), may hold values from 0 to 255, as said below
- block_counts: int32 [256], P('beam'), may hold values from 1 to 4
- out_weight: bfloat16 [8192, 8192], P('head', 'beam'), may hold values from -0.0625 to 0.0625
Outputs:
- mixed: bfloat16 [256, 8192], P('head', 'beam')
The draws below stay inside these ranges and needn't reach their ends.
Inputs may be any that keep to these rules, and one draw needn't show every extreme that they name: Every beam's parent belongs to the same request: parents[b] // 16 == b // 16.
All inputs are finite; a program needn't handle non-finite values.
Results may differ from the reference program's by a relative error of at most 0.0049.
Values may be sent and summed in bfloat16 or wider, within the bound.
A program may use at most 64 MiB of HBM per device.

```python
import math
import jax
import jax.numpy as jnp
from jax import lax

D = 8192
HQ = 64
KVH = 8
HD = 128
QPK = 8
BEAM_WIDTH = 16
BEAMS = 256
REQUESTS = 16
PROMPT = 16384
BLOCK_LEN = 128
BLOCKS = 4
PRIV = 512


def base_queries(key):
    return jax.random.normal(key, (BEAMS, HQ * HD), jnp.float32)


def base_prompt(key):
    return 2.5 * jax.random.normal(jax.random.fold_in(key, 101), (REQUESTS, PROMPT, KVH * HD), jnp.float32)


def draw_queries(key, part):
    base = base_queries(key)
    return base.astype(jnp.bfloat16)


def draw_new_keys(key, part):
    base = base_queries(key)
    key = jax.random.fold_in(key, 3)
    grouped = jnp.mean(base.reshape(BEAMS, KVH, QPK, HD), axis=2).reshape(BEAMS, KVH * HD)
    noise = jax.random.normal(key, (BEAMS, KVH * HD), jnp.float32)
    factor = QPK / math.sqrt(HD) * (2.0 + math.log(PROMPT))
    return (factor * grouped + noise).astype(jnp.bfloat16)


def draw_prompt_keys(key, part):
    prompt = base_prompt(key)
    return prompt.astype(jnp.bfloat16)


def draw_private_keys(key, part):
    key = jax.random.fold_in(key, 6)
    spread = math.sqrt(2.0 * (2.8 + math.log(PROMPT / PRIV)))
    values = spread * jax.random.normal(key, (BEAMS, PRIV, KVH * HD), jnp.float32)
    return jnp.clip(values, -16.0, 16.0).astype(jnp.bfloat16)


def draw_parents(key, part):
    key = jax.random.fold_in(key, 4)
    offsets = jax.random.randint(key, (BEAMS,), 0, BEAM_WIDTH)
    chosen = jnp.arange(BEAMS) // BEAM_WIDTH * BEAM_WIDTH + offsets
    chosen = chosen.at[0].set(0).at[BEAMS - 1].set(BEAMS - 1)
    return chosen.astype(jnp.int32)


def draw_block_counts(key, part):
    key = jax.random.fold_in(key, 5)
    counts = jax.random.randint(key, (BEAMS,), 1, BLOCKS + 1)
    counts = counts.at[0].set(BLOCKS).at[1].set(1)
    return counts.astype(jnp.int32)


def shard_levels(own_key, extent, pieces, low, largest):
    loudness, own = 1.0, jax.random.fold_in(own_key, 6)
    for axis_at, shards_of in pieces:
        draws = jnp.exp(jax.random.uniform(jax.random.fold_in(own, axis_at), (shards_of,), jnp.float32, low / len(pieces), largest / len(pieces)))
        loudness = loudness * jnp.repeat(draws, extent[axis_at] // shards_of).reshape([-1 if axis == axis_at else 1 for axis in range(len(extent))])
    return loudness


def centred(rng, extent, scale, bound, pieces=(), kind=jnp.bfloat16):
    values = scale * jax.random.normal(rng, extent, jnp.float32)
    if pieces:
        values = values * shard_levels(rng, extent, pieces, -0.22, 0.18)
    return jnp.clip(values, -bound, bound).astype(kind)


def setup_inputs(seed: int = 0) -> dict:
    arg_keys = jax.random.split(jax.random.key(seed), 11)
    queries = draw_queries(jax.random.fold_in(arg_keys[10], 71), 0)
    new_keys = draw_new_keys(jax.random.fold_in(arg_keys[10], 71), 0)
    new_values = centred(arg_keys[2], (BEAMS, KVH * HD), 1.0, 6.0, ((0, 64), (1, 8)))
    prompt_keys = draw_prompt_keys(jax.random.fold_in(arg_keys[10], 71), 0)
    prompt_values = centred(arg_keys[4], (REQUESTS, PROMPT, KVH * HD), 1.0, 6.0, ((1, 64), (2, 8)))
    private_keys = draw_private_keys(jax.random.fold_in(arg_keys[10], 71), 0)
    private_values = centred(arg_keys[6], (BEAMS, PRIV, KVH * HD), 1.0, 6.0, ((0, 64), (2, 8)))
    parents = draw_parents(jax.random.fold_in(arg_keys[10], 71), 0)
    block_counts = draw_block_counts(jax.random.fold_in(arg_keys[10], 71), 0)
    out_weight = centred(arg_keys[9], (HQ * HD, D), (HQ * HD) ** -0.5, 0.0625, ((0, 8), (1, 64)))
    return dict(queries=queries, new_keys=new_keys, new_values=new_values, prompt_keys=prompt_keys, prompt_values=prompt_values, private_keys=private_keys, private_values=private_values, parents=parents, block_counts=block_counts, out_weight=out_weight)


masked_score = -1e+30

def reference(queries, new_keys, new_values, prompt_keys, prompt_values, private_keys, private_values, parents, block_counts, out_weight):
    logit_scale = 1.0 / math.sqrt(HD)

    def one_request(request):
        first_beam = (request * BEAM_WIDTH).astype(jnp.int32)
        query_head_count = lax.dynamic_slice_in_dim(queries, first_beam, BEAM_WIDTH, 0).astype(jnp.float32).reshape(BEAM_WIDTH, KVH, QPK, HD)
        beam_self_keys = lax.dynamic_slice_in_dim(new_keys, first_beam, BEAM_WIDTH, 0).astype(jnp.float32).reshape(BEAM_WIDTH, KVH, HD)
        own_values = lax.dynamic_slice_in_dim(new_values, first_beam, BEAM_WIDTH, 0).astype(jnp.float32).reshape(BEAM_WIDTH, KVH, 1, HD)
        prompt_heads = lax.dynamic_index_in_dim(prompt_keys, request, 0, keepdims=False).astype(jnp.float32).reshape(PROMPT, KVH, HD)
        prompt_vals = lax.dynamic_index_in_dim(prompt_values, request, 0, keepdims=False).astype(jnp.float32).reshape(PROMPT, KVH, HD)
        parent_rows = lax.dynamic_slice_in_dim(parents, first_beam, BEAM_WIDTH, 0).astype(jnp.int32)
        cache_keys = jnp.take(private_keys, parent_rows, axis=0).astype(jnp.float32).reshape(BEAM_WIDTH, PRIV, KVH, HD)
        cache_vals = jnp.take(private_values, parent_rows, axis=0).astype(jnp.float32).reshape(BEAM_WIDTH, PRIV, KVH, HD)
        counts = jnp.take(block_counts, parent_rows).astype(jnp.int32)
        prompt_scores = jnp.einsum('bkqd,tkd->bkqt', query_head_count, prompt_heads) * logit_scale
        prompt_max = lax.optimization_barrier(jnp.max(prompt_scores, axis=-1))
        prompt_weights = jnp.exp(prompt_scores - prompt_max[..., None])
        prompt_denominator = lax.optimization_barrier(jnp.sum(prompt_weights, axis=-1))
        rounded = lax.optimization_barrier(prompt_weights.astype(jnp.bfloat16))
        prompt_num = jnp.einsum('bkqt,tkd->bkqd', rounded.astype(jnp.float32), prompt_vals)
        cache_scores = jnp.einsum('bkqd,bpkd->bkqp', query_head_count, cache_keys) * logit_scale
        allowed = jnp.arange(PRIV, dtype=jnp.int32)[None, :] < (counts * BLOCK_LEN)[:, None]
        cache_scores = jnp.where(allowed[:, None, None, :], cache_scores, masked_score)
        private_max = lax.optimization_barrier(jnp.max(cache_scores, axis=-1))
        private_weights = jnp.exp(cache_scores - private_max[..., None])
        private_den = lax.optimization_barrier(jnp.sum(private_weights, axis=-1))
        rounded_private = lax.optimization_barrier(private_weights.astype(jnp.bfloat16))
        private_num = jnp.einsum('bkqp,bpkd->bkqd', rounded_private.astype(jnp.float32), cache_vals)
        beam_self_logit = jnp.einsum('sxjr,sxr->sxj', query_head_count, beam_self_keys) * logit_scale
        overall = jnp.maximum(jnp.maximum(prompt_max, private_max), beam_self_logit)
        first = jnp.exp(prompt_max - overall)
        second = jnp.exp(private_max - overall)
        third = jnp.exp(beam_self_logit - overall)
        numer = first[..., None] * prompt_num + second[..., None] * private_num + third[..., None] * own_values
        denom = first * prompt_denominator + second * private_den + third
        return (numer / denom[..., None]).astype(jnp.bfloat16).reshape(BEAM_WIDTH, KVH * QPK * HD)
    attended = lax.map(one_request, jnp.arange(REQUESTS, dtype=jnp.int32)).reshape(BEAMS, HQ * HD)
    return jnp.dot(attended, out_weight, preferred_element_type=jnp.float32).astype(jnp.bfloat16)
```

```python
import functools
import math

import jax
import jax.numpy as jnp
from jax import lax
from jax.experimental import pallas as pl
from jax.experimental.pallas import tpu as pltpu
from jax.sharding import PartitionSpec as P

MESH = pl.DeviceIdType.MESH
HD = 128
QPK = 8
OWN_BEAMS = 4
BLOCK_LEN = 128
PRIV = 512
NX, NZ, NY = 4, 8, 8
CHIPS = NX * NZ
SET = 8
SLOTS = CHIPS + 4
TO_LOG2 = 1.0 / math.sqrt(HD) / math.log(2.0)
LOWEST = -3.0e38
LAST = (((1,), (1,)), ((), ()))


def kernel(
    queries, new_keys, new_values, prompt_keys, prompt_values, private_keys, private_values, parents, counts, weight,
    out_ref,
    q_in, nk_in, nv_in, par_in, cnt_in, q_rows, q_mine, q_set, q_own, par_mine, par_all,
    keys, values, values_t, pkeys, pvalues, pvalues_t, self_rows, pscores, w_both,
    num_out, stat_out, num_in, stat_in, att_mine, att_all, part, part_in,
    small_sem, kv_sem, priv_sem, w_sem, pair_send, pair_recv,
    q_send, q_recv, own_send, own_recv, par_send, par_recv,
    num_send, num_recv, stat_send, stat_recv, att_send, att_recv, part_send, part_recv,
):
    d = lax.axis_index("beam")
    y = lax.axis_index("head")
    core = d % 2
    chip = d // 2
    x = chip // NZ
    z = chip % NZ
    request = chip // 2
    home = request // SET
    slot = request % SET
    member = d % 4

    barrier = pltpu.get_barrier_semaphore()

    def greet_plane(k, carry):
        pl.semaphore_signal(barrier, inc=1, device_id=((d + k) % 64, y), device_id_type=MESH)
        return carry

    def greet_column(k, carry):
        pl.semaphore_signal(barrier, inc=1, device_id=(chip * 2 + k % 2, (y + 1 + k // 2) % NY), device_id_type=MESH)
        return carry

    lax.fori_loop(1, 64, greet_plane, 0)
    lax.fori_loop(0, 14, greet_column, 0)

    small = [
        pltpu.make_async_copy(src, dst, small_sem.at[n])
        for n, (src, dst) in enumerate(
            ((queries, q_in), (new_keys, nk_in), (new_values, nv_in), (parents, par_in), (counts, cnt_in))
        )
    ]
    for copy in small:
        copy.start()
    private = [
        pltpu.make_async_copy(private_keys, pkeys, priv_sem.at[0]),
        pltpu.make_async_copy(private_values, pvalues, priv_sem.at[1]),
    ]
    for copy in private:
        copy.start()
    mine = pl.ds(core * SET, SET)
    theirs = pl.ds((1 - core) * SET, SET)
    cached = [
        pltpu.make_async_copy(prompt_keys.at[mine], keys.at[:, 0], kv_sem.at[0]),
        pltpu.make_async_copy(prompt_values.at[mine], values.at[:, 0], kv_sem.at[1]),
    ]
    for copy in cached:
        copy.start()
    own_weight = pltpu.make_async_copy(weight, w_both.at[core], w_sem.at[0])
    own_weight.start()
    pair = (chip * 2 + 1 - core, y)
    swaps = [
        pltpu.make_async_remote_copy(
            src, dst, pair_send.at[n], pair_recv.at[n], device_id=pair, device_id_type=MESH
        )
        for n, (src, dst) in enumerate(
            (
                (prompt_keys.at[theirs], keys.at[:, 1]),
                (prompt_values.at[theirs], values.at[:, 1]),
                (weight, w_both.at[core]),
            )
        )
    ]

    small[0].wait()
    q_wide = q_in[...].astype(jnp.float32)
    for head in range(QPK):
        q_rows[pl.ds(head * OWN_BEAMS, OWN_BEAMS), :] = q_wide[:, head * HD : (head + 1) * HD]
    q_mine[...] = q_rows[...].astype(jnp.bfloat16)
    lane = lax.broadcasted_iota(jnp.int32, (8, HD), 1)
    small[3].wait()
    row_parent = jnp.zeros((8, HD), jnp.int32)
    for beam in range(OWN_BEAMS):
        row_parent = jnp.where(lane % OWN_BEAMS == beam, par_in[beam], row_parent)
    par_mine[...] = jnp.where(lane // 32 == member, row_parent, 0)

    pl.semaphore_wait(barrier, 77)

    def own_copy(j):
        to = (request * 4 + j, y)
        return (
            pltpu.make_async_remote_copy(
                q_mine, q_own.at[member], own_send.at[j], own_recv.at[0], device_id=to, device_id_type=MESH
            ),
            pltpu.make_async_remote_copy(
                par_mine, par_all.at[member], par_send.at[j], par_recv.at[0], device_id=to, device_id_type=MESH
            ),
        )

    def own_start(j, carry):
        @pl.when(j != member)
        def _():
            for copy in own_copy(j):
                copy.start()

        return carry

    def own_done(j, carry):
        @pl.when(j != member)
        def _():
            for copy in own_copy(j):
                copy.wait_send()

        return carry

    lax.fori_loop(0, 4, own_start, 0)
    pltpu.make_async_copy(q_mine, q_own.at[member], own_recv.at[0]).start()
    pltpu.make_async_copy(par_mine, par_all.at[member], par_recv.at[0]).start()

    def q_target(n):
        return (4 * ((slot - n // 4 + 8) % 8) + (chip + n) % 4) * 2 + home

    def q_copy(n):
        return pltpu.make_async_remote_copy(
            q_mine, q_set.at[slot, member], q_send.at[n], q_recv.at[slot], device_id=(q_target(n), y), device_id_type=MESH
        )

    def q_start(n, carry):
        @pl.when(q_target(n) != d)
        def _():
            q_copy(n).start()

        return carry

    def q_done(n, carry):
        @pl.when(q_target(n) != d)
        def _():
            q_copy(n).wait_send()

        return carry

    lax.fori_loop(0, CHIPS, q_start, 0)

    @pl.when(home == core)
    def _():
        pltpu.make_async_copy(q_mine, q_set.at[slot, member], q_recv.at[slot]).start()

    for copy in swaps:
        copy.start()

    private[1].wait()

    def turn_private(j, carry):
        pvalues_t[j] = pvalues[j].T
        return carry

    lax.fori_loop(0, OWN_BEAMS, turn_private, 0)
    small[1].wait()
    small[2].wait()
    small[4].wait()
    self_rows[...] = jnp.zeros_like(self_rows)
    self_rows[0, pl.ds(0, OWN_BEAMS), :] = nk_in[...].astype(jnp.float32)
    self_rows[1, pl.ds(0, OWN_BEAMS), :] = nv_in[...].astype(jnp.float32)
    self_keys = self_rows[0].astype(jnp.bfloat16)
    self_values_t = self_rows[1].T.astype(jnp.bfloat16)

    private[0].wait()
    pltpu.make_async_copy(q_own, q_own, own_recv.at[0]).wait()
    pltpu.make_async_copy(par_all, par_all, par_recv.at[0]).wait()
    q_request = q_own[...].reshape(128, HD)
    row_parent = par_all[0] + par_all[1] + par_all[2] + par_all[3]
    row_parent = row_parent[0:1, :]
    position = lax.broadcasted_iota(jnp.int32, (PRIV, HD), 0)
    at = lax.broadcasted_iota(jnp.int32, (HD, HD), 0)
    across = lax.broadcasted_iota(jnp.int32, (HD, HD), 1)
    scores = lax.dot_general(self_keys, q_request, LAST, preferred_element_type=jnp.float32) * TO_LOG2
    is_own = jnp.logical_and(across // 32 == member, across % OWN_BEAMS == at)
    self_scores = jnp.where(is_own, scores, LOWEST)

    def private_scores(j, highest):
        got = lax.dot_general(pkeys[j], q_request, LAST, preferred_element_type=jnp.float32) * TO_LOG2
        filled = jnp.where(row_parent == d * OWN_BEAMS + j, cnt_in[j] * BLOCK_LEN, 0)
        got = jnp.where(position < filled, got, LOWEST)
        pscores[j] = got
        return jnp.maximum(highest, jnp.max(got, axis=0, keepdims=True))

    highest = lax.fori_loop(0, OWN_BEAMS, private_scores, jnp.max(self_scores, axis=0, keepdims=True))
    weights = jnp.where(self_scores > LOWEST, jnp.exp2(self_scores - highest), 0.0)
    total = jnp.sum(weights, axis=0, keepdims=True)
    summed = jnp.dot(self_values_t, weights.astype(jnp.bfloat16), preferred_element_type=jnp.float32)

    def private_sums(j, carry):
        total, summed = carry
        got = pscores[j]
        weights = jnp.where(got > LOWEST, jnp.exp2(got - highest), 0.0)
        total = total + jnp.sum(weights, axis=0, keepdims=True)
        summed = summed + jnp.dot(pvalues_t[j], weights.astype(jnp.bfloat16), preferred_element_type=jnp.float32)
        return total, summed

    total, summed = lax.fori_loop(0, OWN_BEAMS, private_sums, (total, summed))
    num_out[SET] = summed.astype(jnp.bfloat16)
    stat_out[SET, 0:1, :] = highest
    stat_out[SET, 1:2, :] = total

    def result_copies(source, owner_slot, to_core, into, n, quarter):
        owner = 4 * owner_slot + quarter
        rows = pl.ds(pl.multiple_of(quarter * 32, 32), 32)
        to = (owner * 2 + to_core, y)
        return (
            to[0] != d,
            (
                pltpu.make_async_remote_copy(
                    num_out.at[source, rows], num_in.at[into], num_send.at[n], num_recv.at[0],
                    device_id=to, device_id_type=MESH,
                ),
                pltpu.make_async_remote_copy(
                    stat_out.at[source], stat_in.at[into], stat_send.at[n], stat_recv.at[0],
                    device_id=to, device_id_type=MESH,
                ),
            ),
            (
                pltpu.make_async_copy(num_out.at[source, rows], num_in.at[into], num_recv.at[0]),
                pltpu.make_async_copy(stat_out.at[source], stat_in.at[into], stat_recv.at[0]),
            ),
        )

    def prompt_result(n):
        owner_slot = (chip // 4 + n // 4) % SET
        return result_copies(owner_slot, owner_slot, core, chip, n, (chip + n) % 4)

    def private_result(j):
        return result_copies(SET, slot, home, CHIPS + member, CHIPS + j, (chip + j) % 4)

    def result_start(make, n):
        remote, far, near = make(n)

        @pl.when(remote)
        def _():
            for copy in far:
                copy.start()

        @pl.when(jnp.logical_not(remote))
        def _():
            for copy in near:
                copy.start()

    def result_done(make, n):
        remote, far, _ = make(n)

        @pl.when(remote)
        def _():
            for copy in far:
                copy.wait_send()

    def private_start(j, carry):
        result_start(private_result, j)
        return carry

    lax.fori_loop(0, 4, private_start, 0)

    for copy in cached:
        copy.wait()
    for copy in swaps[:2]:
        copy.wait_recv()

    def turn(i, carry):
        values_t[i] = values[i].reshape(512, HD).T
        return carry

    lax.fori_loop(0, SET, turn, 0)

    def one_request(s, carry):
        i = (chip // 4 + s) % SET
        pltpu.make_async_copy(q_set.at[i], q_set.at[i], q_recv.at[i]).wait()
        rows = q_set[i].reshape(128, HD)
        scores = (
            lax.dot_general(keys[i].reshape(512, HD), rows, LAST, preferred_element_type=jnp.float32) * TO_LOG2
        )
        highest = jnp.max(scores, axis=0, keepdims=True)
        weights = jnp.exp2(scores - highest)
        stat_out[i, 0:1, :] = highest
        stat_out[i, 1:2, :] = jnp.sum(weights, axis=0, keepdims=True)
        num_out[i] = jnp.dot(
            values_t[i], weights.astype(jnp.bfloat16), preferred_element_type=jnp.float32
        ).astype(jnp.bfloat16)
        for j in range(4):
            result_start(prompt_result, s * 4 + j)
        return carry

    lax.fori_loop(0, SET, one_request, 0)

    lax.fori_loop(0, 4, own_done, 0)
    lax.fori_loop(0, CHIPS, q_done, 0)
    for copy in swaps:
        copy.wait_send()

    pltpu.make_async_copy(stat_in, stat_in, stat_recv.at[0]).wait()
    stats = [stat_in[k] for k in range(SLOTS)]
    highest = stats[0][0:1, :]
    for k in range(1, SLOTS):
        highest = jnp.maximum(highest, stats[k][0:1, :])
    shares = [jnp.exp2(stats[k][0:1, :] - highest) for k in range(SLOTS)]
    total = shares[0] * stats[0][1:2, :]
    for k in range(1, SLOTS):
        total = total + shares[k] * stats[k][1:2, :]
    pltpu.make_async_copy(num_in, num_in, num_recv.at[0]).wait()
    summed = shares[0] * num_in[0].astype(jnp.float32)
    for k in range(1, SLOTS):
        summed = summed + shares[k] * num_in[k].astype(jnp.float32)
    attended = (summed / total).astype(jnp.bfloat16).astype(jnp.float32)

    head_of = lax.broadcasted_iota(jnp.int32, (32, HD), 1) // OWN_BEAMS % QPK
    spread = jnp.concatenate(
        [jnp.where(head_of == head, attended, 0.0).astype(jnp.bfloat16) for head in range(QPK)], axis=0
    )
    beam_at = lax.broadcasted_iota(jnp.int32, (16, HD), 0)
    beam_lane = lax.broadcasted_iota(jnp.int32, (16, HD), 1)
    chosen = (beam_lane // 32 * OWN_BEAMS + beam_lane % OWN_BEAMS == beam_at).astype(jnp.float32)
    att_mine[...] = lax.dot_general(
        chosen.astype(jnp.bfloat16), spread, LAST, preferred_element_type=jnp.float32
    ).astype(jnp.bfloat16)

    place = att_all.at[chip % 4, chip // 4]

    def att_copy(k):
        to = ((((x + k // NZ) % NX) * NZ + (z + k) % NZ) * 2 + core, y)
        return pltpu.make_async_remote_copy(
            att_mine, place, att_send.at[k], att_recv.at[0], device_id=to, device_id_type=MESH
        )

    def att_start(k, carry):
        att_copy(k).start()
        return carry

    def att_done(k, carry):
        att_copy(k).wait_send()
        return carry

    lax.fori_loop(1, CHIPS, att_start, 0)
    pltpu.make_async_copy(att_mine, place, att_recv.at[0]).start()

    def prompt_done(n, carry):
        result_done(prompt_result, n)
        return carry

    def private_done(n, carry):
        result_done(private_result, n)
        return carry

    lax.fori_loop(0, CHIPS, prompt_done, 0)
    lax.fori_loop(0, 4, private_done, 0)
    own_weight.wait()
    swaps[2].wait_recv()

    pltpu.make_async_copy(att_all, att_all, att_recv.at[0]).wait()
    rows = [att_all[quarter].reshape(128, 256) for quarter in range(4)]
    for side in range(2):
        product = jnp.zeros((128, HD), jnp.float32)
        for quarter in range(4):
            product = product + jnp.dot(
                rows[quarter], w_both[side, :, quarter].reshape(256, HD), preferred_element_type=jnp.float32
            )
        part[side] = product.astype(jnp.bfloat16).reshape(4, 32, HD)

    def part_target(n):
        return chip * 2 + n % 2, core * 4 + (y + n // 2) % 4

    def part_copy(n):
        to = part_target(n)
        return pltpu.make_async_remote_copy(
            part.at[n % 2, (y + n // 2) % 4], part_in.at[y], part_send.at[n], part_recv.at[0],
            device_id=to, device_id_type=MESH,
        )

    def part_is_far(n):
        to = part_target(n)
        return jnp.logical_or(to[0] != d, to[1] != y)

    def part_start(n, carry):
        @pl.when(part_is_far(n))
        def _():
            part_copy(n).start()

        return carry

    def part_done(n, carry):
        @pl.when(part_is_far(n))
        def _():
            part_copy(n).wait_send()

        return carry

    lax.fori_loop(0, 8, part_start, 0)

    @pl.when(y // 4 == core)
    def _():
        pltpu.make_async_copy(part.at[core, y % 4], part_in.at[y], part_recv.at[0]).start()

    lax.fori_loop(1, CHIPS, att_done, 0)
    pltpu.make_async_copy(part_in, part_in, part_recv.at[0]).wait()
    mixed = part_in[0].astype(jnp.float32)
    for k in range(1, NY):
        mixed = mixed + part_in[k].astype(jnp.float32)
    out_ref[...] = mixed.astype(jnp.bfloat16)
    lax.fori_loop(0, 8, part_done, 0)


def per_device(
    queries, new_keys, new_values, prompt_keys, prompt_values, private_keys, private_values, parents, counts, weight
):
    bf16, f32, i32 = jnp.bfloat16, jnp.float32, jnp.int32
    dma = pltpu.SemaphoreType.DMA
    anywhere = pl.BlockSpec(memory_space=pl.ANY)
    return pl.pallas_call(
        kernel,
        out_shape=jax.ShapeDtypeStruct((32, HD), bf16),
        in_specs=[anywhere] * 10,
        out_specs=pl.BlockSpec(memory_space=pltpu.VMEM),
        scratch_shapes=[
            pltpu.VMEM((OWN_BEAMS, QPK * HD), bf16),
            pltpu.VMEM((OWN_BEAMS, HD), bf16),
            pltpu.VMEM((OWN_BEAMS, HD), bf16),
            pltpu.SMEM((OWN_BEAMS,), i32),
            pltpu.SMEM((OWN_BEAMS,), i32),
            pltpu.VMEM((32, HD), f32),
            pltpu.VMEM((32, HD), bf16),
            pltpu.VMEM((SET, 4, 32, HD), bf16),
            pltpu.VMEM((4, 32, HD), bf16),
            pltpu.VMEM((8, HD), i32),
            pltpu.VMEM((4, 8, HD), i32),
            pltpu.VMEM((SET, 2, 256, HD), bf16),
            pltpu.VMEM((SET, 2, 256, HD), bf16),
            pltpu.VMEM((SET, HD, 512), bf16),
            pltpu.VMEM((OWN_BEAMS, PRIV, HD), bf16),
            pltpu.VMEM((OWN_BEAMS, PRIV, HD), bf16),
            pltpu.VMEM((OWN_BEAMS, HD, PRIV), bf16),
            pltpu.VMEM((2, HD, HD), f32),
            pltpu.VMEM((OWN_BEAMS, PRIV, HD), f32),
            pltpu.VMEM((2, QPK, 4, 32, HD), bf16),
            pltpu.VMEM((SET + 1, HD, HD), bf16),
            pltpu.VMEM((SET + 1, 2, HD), f32),
            pltpu.VMEM((SLOTS, 32, HD), bf16),
            pltpu.VMEM((SLOTS, 2, HD), f32),
            pltpu.VMEM((16, 256), bf16),
            pltpu.VMEM((4, SET, 16, 256), bf16),
            pltpu.VMEM((2, 4, 32, HD), bf16),
            pltpu.VMEM((NY, 32, HD), bf16),
            dma((5,)), dma((2,)), dma((2,)), dma((1,)), dma((3,)), dma((3,)),
            dma((CHIPS,)), dma((SET,)), dma((4,)), dma((1,)), dma((4,)), dma((1,)),
            dma((SLOTS,)), dma((1,)), dma((SLOTS,)), dma((1,)), dma((CHIPS,)), dma((1,)), dma((8,)), dma((1,)),
        ],
        compiler_params=pltpu.CompilerParams(
            collective_id=0, has_side_effects=True, vmem_limit_bytes=48 << 20
        ),
    )(
        queries, new_keys, new_values, prompt_keys, prompt_values, private_keys, private_values, parents, counts,
        weight.reshape(QPK, 4, 32, HD),
    )


def solution(mesh):
    placed = (
        P("beam", "head"),
        P("beam", "head"),
        P("beam", "head"),
        P(None, "beam", "head"),
        P(None, "beam", "head"),
        P("beam", None, "head"),
        P("beam", None, "head"),
        P("beam"),
        P("beam"),
        P("head", "beam"),
    )
    return jax.shard_map(per_device, mesh=mesh, in_specs=placed, out_specs=P("head", "beam"), check_vma=False)
```

```python
import math

import jax
import jax.numpy as jnp
from jax import lax
from jax.experimental import pallas as pl
from jax.experimental.pallas import tpu as pltpu
from jax.sharding import PartitionSpec as P

MESH = pl.DeviceIdType.MESH
HD = 128
QPK = 8
OWN_BEAMS = 4
BLOCK_LEN = 128
PRIV = 512
NX, NZ, NY = 4, 8, 8
CHIPS = NX * NZ
SET = 8
SLOTS = CHIPS + 4
TO_LOG2 = 1.0 / math.sqrt(HD) / math.log(2.0)
LOWEST = -3.0e38
LAST = (((1,), (1,)), ((), ()))


def kernel(
    queries, new_keys, new_values, prompt_keys, prompt_values, private_keys, private_values, parents, counts, weight,
    out_ref,
    q_in, nk_in, nv_in, par_in, cnt_in, q_rows, q_mine, q_set, q_own, par_mine, par_all,
    keys, values, values_t, pkeys, pvalues, pvalues_t, self_rows, pscores, w_both,
    num_out, stat_out, num_in, stat_in, att_mine, att_all, part, part_in,
    small_sem, kv_sem, priv_sem, w_sem, pair_send, pair_recv,
    q_send, q_recv, own_send, own_recv, par_send, par_recv,
    num_send, num_recv, stat_send, stat_recv, att_send, att_recv, part_send, part_recv,
):
    d = lax.axis_index("beam")
    y = lax.axis_index("head")
    core = d % 2
    chip = d // 2
    x = chip // NZ
    z = chip % NZ
    request = chip // 2
    home = request // SET
    slot = request % SET
    member = d % 4

    def far_first(k):
        u, t = k % NX, k // NX
        return (2 + (u + 1) // 2 * (1 - 2 * (u % 2))) % NX, (4 + (t + 1) // 2 * (1 - 2 * (t % 2))) % NZ

    def same_core(k):
        dx, dz = far_first(k)
        return (((x + dx) % NX) * NZ + (z + dz) % NZ) * 2 + core, y

    small = [
        pltpu.make_async_copy(src, dst, small_sem.at[n])
        for n, (src, dst) in enumerate(
            ((queries, q_in), (new_keys, nk_in), (new_values, nv_in), (parents, par_in), (counts, cnt_in))
        )
    ]
    for copy in small:
        copy.start()
    barrier = pltpu.get_barrier_semaphore()

    def tell(to):
        pl.semaphore_signal(barrier, inc=1, device_id=to, device_id_type=MESH)

    def tell_same(k, carry):
        tell(same_core(k))
        return carry

    def tell_other(k, carry):
        tell(((core * 16 + (chip + 8 + k) % 16) * 2 + 1 - core, y))
        return carry

    def tell_column(k, carry):
        to = (y + 4 + k) % NY
        row = chip * 2 + y // 4

        @pl.when(jnp.logical_or(row != d, to != y))
        def _():
            tell((row, to))

        return carry

    lax.fori_loop(0, CHIPS - 1, tell_same, 0, unroll=True)
    lax.fori_loop(0, 16, tell_other, 0, unroll=True)
    lax.fori_loop(0, NY, tell_column, 0, unroll=True)

    @pl.when(home != core)
    def _():
        tell((chip * 2 + 1 - core, y))
        tell(((chip + 1 - 2 * (chip % 2)) * 2 + 1 - core, y))

    private = [
        pltpu.make_async_copy(private_keys, pkeys, priv_sem.at[0]),
        pltpu.make_async_copy(private_values, pvalues, priv_sem.at[1]),
    ]
    for copy in private:
        copy.start()
    mine = pl.ds(core * SET, SET)
    theirs = pl.ds((1 - core) * SET, SET)
    cached = [
        pltpu.make_async_copy(prompt_keys.at[mine], keys.at[:, 0], kv_sem.at[0]),
        pltpu.make_async_copy(prompt_values.at[mine], values.at[:, 0], kv_sem.at[1]),
    ]
    for copy in cached:
        copy.start()
    own_weight = pltpu.make_async_copy(weight, w_both.at[core], w_sem.at[0])
    own_weight.start()
    pair = (chip * 2 + 1 - core, y)
    swaps = [
        pltpu.make_async_remote_copy(
            src, dst, pair_send.at[n], pair_recv.at[n], device_id=pair, device_id_type=MESH
        )
        for n, (src, dst) in enumerate(
            (
                (prompt_keys.at[theirs], keys.at[:, 1]),
                (prompt_values.at[theirs], values.at[:, 1]),
                (weight, w_both.at[core]),
            )
        )
    ]

    small[0].wait()
    q_wide = q_in[...].astype(jnp.float32)
    for head in range(QPK):
        q_rows[pl.ds(head * OWN_BEAMS, OWN_BEAMS), :] = q_wide[:, head * HD : (head + 1) * HD]
    q_mine[...] = q_rows[...].astype(jnp.bfloat16)
    lane = lax.broadcasted_iota(jnp.int32, (8, HD), 1)
    small[3].wait()
    row_parent = jnp.zeros((8, HD), jnp.int32)
    for beam in range(OWN_BEAMS):
        row_parent = jnp.where(lane % OWN_BEAMS == beam, par_in[beam], row_parent)
    par_mine[...] = jnp.where(lane // 32 == member, row_parent, 0)

    pl.semaphore_wait(barrier, jnp.where(home == core, 33, 63) + jnp.where(y // 4 == core, 7, 8))

    def own_copy(j):
        to = (request * 4 + j, y)
        return (
            pltpu.make_async_remote_copy(
                q_mine, q_own.at[member], own_send.at[0], own_recv.at[0], device_id=to, device_id_type=MESH
            ),
            pltpu.make_async_remote_copy(
                par_mine, par_all.at[member], par_send.at[0], par_recv.at[0], device_id=to, device_id_type=MESH
            ),
        )

    def own_start(j, carry):
        @pl.when(j != member)
        def _():
            for copy in own_copy(j):
                copy.start()

        return carry

    def sent(blocks, sem, count):
        pltpu.make_async_copy(blocks.at[pl.ds(0, count)], blocks.at[pl.ds(0, count)], sem.at[0]).wait()

    def sent_either(blocks, sem, fewer, count):
        @pl.when(fewer)
        def _():
            sent(blocks, sem, count - 1)

        @pl.when(jnp.logical_not(fewer))
        def _():
            sent(blocks, sem, count)

    lax.fori_loop(0, 4, own_start, 0, unroll=True)
    pltpu.make_async_copy(q_mine, q_own.at[member], own_recv.at[0]).start()
    pltpu.make_async_copy(par_mine, par_all.at[member], par_recv.at[0]).start()

    def turn_x(s):
        u = s // 2
        return (2 + (u + 1) // 2 * (1 - 2 * (u % 2))) % NX

    def q_target(n):
        to_x = (slot // 2 - turn_x(n // 4) + NX) % NX
        to_z = 4 * ((slot + 1 + n // 4) % 2) + (z + n) % 4
        return (to_x * NZ + to_z) * 2 + home

    def q_copy(n):
        return pltpu.make_async_remote_copy(
            q_mine, q_set.at[slot, member], q_send.at[0], q_recv.at[slot], device_id=(q_target(n), y), device_id_type=MESH
        )

    def q_start(n, carry):
        @pl.when(q_target(n) != d)
        def _():
            q_copy(n).start()

        return carry

    lax.fori_loop(0, CHIPS, q_start, 0, unroll=True)

    @pl.when(home == core)
    def _():
        pltpu.make_async_copy(q_mine, q_set.at[slot, member], q_recv.at[slot]).start()

    for copy in swaps:
        copy.start()

    private[1].wait()

    def turn_private(j, carry):
        pvalues_t[j] = pvalues[j].T
        return carry

    lax.fori_loop(0, OWN_BEAMS, turn_private, 0, unroll=True)
    cached[1].wait()

    def turn_mine(i, carry):
        values_t[i, :, 0:256] = values[i, 0].T
        return carry

    lax.fori_loop(0, SET, turn_mine, 0, unroll=2)
    small[1].wait()
    small[2].wait()
    small[4].wait()
    self_rows[...] = jnp.zeros_like(self_rows)
    self_rows[0, pl.ds(0, OWN_BEAMS), :] = nk_in[...].astype(jnp.float32)
    self_rows[1, pl.ds(0, OWN_BEAMS), :] = nv_in[...].astype(jnp.float32)
    self_keys = self_rows[0].astype(jnp.bfloat16)
    self_values_t = self_rows[1].T.astype(jnp.bfloat16)

    private[0].wait()
    pltpu.make_async_copy(q_own, q_own, own_recv.at[0]).wait()
    pltpu.make_async_copy(par_all, par_all, par_recv.at[0]).wait()
    q_request = q_own[...].reshape(128, HD)
    row_parent = par_all[0] + par_all[1] + par_all[2] + par_all[3]
    row_parent = row_parent[0:1, :]
    position = lax.broadcasted_iota(jnp.int32, (PRIV, HD), 0)
    at = lax.broadcasted_iota(jnp.int32, (HD, HD), 0)
    across = lax.broadcasted_iota(jnp.int32, (HD, HD), 1)
    scores = lax.dot_general(self_keys, q_request, LAST, preferred_element_type=jnp.float32) * TO_LOG2
    is_own = jnp.logical_and(across // 32 == member, across % OWN_BEAMS == at)
    self_scores = jnp.where(is_own, scores, LOWEST)

    def private_scores(j, highest):
        got = lax.dot_general(pkeys[j], q_request, LAST, preferred_element_type=jnp.float32) * TO_LOG2
        filled = jnp.where(row_parent == d * OWN_BEAMS + j, cnt_in[j] * BLOCK_LEN, 0)
        got = jnp.where(position < filled, got, LOWEST)
        pscores[j] = got
        return jnp.maximum(highest, jnp.max(got, axis=0, keepdims=True))

    highest = lax.fori_loop(
        0, OWN_BEAMS, private_scores, jnp.max(self_scores, axis=0, keepdims=True), unroll=True
    )
    weights = jnp.where(self_scores > LOWEST, jnp.exp2(self_scores - highest), 0.0)
    total = jnp.sum(weights, axis=0, keepdims=True)
    summed = jnp.dot(self_values_t, weights.astype(jnp.bfloat16), preferred_element_type=jnp.float32)

    def private_sums(j, carry):
        total, summed = carry
        got = pscores[j]
        weights = jnp.where(got > LOWEST, jnp.exp2(got - highest), 0.0)
        total = total + jnp.sum(weights, axis=0, keepdims=True)
        summed = summed + jnp.dot(pvalues_t[j], weights.astype(jnp.bfloat16), preferred_element_type=jnp.float32)
        return total, summed

    total, summed = lax.fori_loop(0, OWN_BEAMS, private_sums, (total, summed), unroll=True)
    num_out[SET] = summed.astype(jnp.bfloat16)
    stat_out[SET, 0:1, :] = highest
    stat_out[SET, 1:2, :] = total

    def result_copies(source, owner_slot, to_core, into, n, quarter):
        owner = 4 * owner_slot + quarter
        rows = pl.ds(pl.multiple_of(quarter * 32, 32), 32)
        to = (owner * 2 + to_core, y)
        return (
            to[0] != d,
            (
                pltpu.make_async_remote_copy(
                    num_out.at[source, rows], num_in.at[into], num_send.at[0], num_recv.at[0],
                    device_id=to, device_id_type=MESH,
                ),
                pltpu.make_async_remote_copy(
                    stat_out.at[source], stat_in.at[into], stat_send.at[0], stat_recv.at[0],
                    device_id=to, device_id_type=MESH,
                ),
            ),
            (
                pltpu.make_async_copy(num_out.at[source, rows], num_in.at[into], num_recv.at[0]),
                pltpu.make_async_copy(stat_out.at[source], stat_in.at[into], stat_recv.at[0]),
            ),
        )

    def nth_request(s):
        return 2 * ((x + turn_x(s)) % NX) + (z // 4 + 1 + s) % 2

    def prompt_result(n):
        owner_slot = nth_request(n // 4)
        return result_copies(owner_slot, owner_slot, core, chip, n, (chip + n) % 4)

    def private_result(j):
        return result_copies(SET, slot, home, CHIPS + member, CHIPS + j, (chip + j) % 4)

    def result_start(make, n):
        remote, far, near = make(n)

        @pl.when(remote)
        def _():
            for copy in far:
                copy.start()

        @pl.when(jnp.logical_not(remote))
        def _():
            for copy in near:
                copy.start()

    def private_start(j, carry):
        result_start(private_result, j)
        return carry

    lax.fori_loop(0, 4, private_start, 0, unroll=True)

    cached[0].wait()
    for copy in swaps[:2]:
        copy.wait_recv()

    def turn_swapped(i, carry):
        values_t[i, :, 256:512] = values[i, 1].T
        return carry

    lax.fori_loop(0, SET, turn_swapped, 0, unroll=2)

    def two_requests(pair_at, carry):
        some = [nth_request(pair_at * 2), nth_request(pair_at * 2 + 1)]
        for i in some:
            pltpu.make_async_copy(q_set.at[i], q_set.at[i], q_recv.at[i]).wait()
        done = []
        for i in some:
            rows = q_set[i].reshape(128, HD)
            scores = (
                lax.dot_general(keys[i].reshape(512, HD), rows, LAST, preferred_element_type=jnp.float32) * TO_LOG2
            )
            highest = jnp.max(scores, axis=0, keepdims=True)
            weights = jnp.exp2(scores - highest)
            total = jnp.sum(weights, axis=0, keepdims=True)
            summed = jnp.dot(values_t[i], weights.astype(jnp.bfloat16), preferred_element_type=jnp.float32)
            done.append((highest, total, summed.astype(jnp.bfloat16)))
        for i, (highest, total, summed) in zip(some, done, strict=True):
            stat_out[i, 0:1, :] = highest
            stat_out[i, 1:2, :] = total
            num_out[i] = summed
        for j in range(8):
            result_start(prompt_result, pair_at * 8 + j)
        return carry

    lax.fori_loop(0, SET // 2, two_requests, 0, unroll=True)

    sent(q_own, own_send, 3)
    sent(par_all, par_send, 3)
    sent_either(num_in, q_send, home == core, CHIPS)
    for copy in swaps:
        copy.wait_send()

    pltpu.make_async_copy(stat_in, stat_in, stat_recv.at[0]).wait()
    stats = [stat_in[k] for k in range(SLOTS)]
    highest = stats[0][0:1, :]
    for k in range(1, SLOTS):
        highest = jnp.maximum(highest, stats[k][0:1, :])
    shares = [jnp.exp2(stats[k][0:1, :] - highest) for k in range(SLOTS)]
    total = shares[0] * stats[0][1:2, :]
    for k in range(1, SLOTS):
        total = total + shares[k] * stats[k][1:2, :]
    pltpu.make_async_copy(num_in, num_in, num_recv.at[0]).wait()
    summed = shares[0] * num_in[0].astype(jnp.float32)
    for k in range(1, SLOTS):
        summed = summed + shares[k] * num_in[k].astype(jnp.float32)
    attended = (summed / total).astype(jnp.bfloat16).astype(jnp.float32)

    head_of = lax.broadcasted_iota(jnp.int32, (32, HD), 1) // OWN_BEAMS % QPK
    spread = jnp.concatenate(
        [jnp.where(head_of == head, attended, 0.0).astype(jnp.bfloat16) for head in range(QPK)], axis=0
    )
    beam_at = lax.broadcasted_iota(jnp.int32, (16, HD), 0)
    beam_lane = lax.broadcasted_iota(jnp.int32, (16, HD), 1)
    chosen = (beam_lane // 32 * OWN_BEAMS + beam_lane % OWN_BEAMS == beam_at).astype(jnp.float32)
    att_mine[...] = lax.dot_general(
        chosen.astype(jnp.bfloat16), spread, LAST, preferred_element_type=jnp.float32
    ).astype(jnp.bfloat16)

    place = att_all.at[chip % 4, chip // 4]

    def att_copy(k):
        return pltpu.make_async_remote_copy(
            att_mine, place, att_send.at[0], att_recv.at[0], device_id=same_core(k), device_id_type=MESH
        )

    def att_start(k, carry):
        att_copy(k).start()
        return carry

    lax.fori_loop(0, CHIPS - 1, att_start, 0, unroll=True)
    pltpu.make_async_copy(att_mine, place, att_recv.at[0]).start()

    kept = jnp.logical_and(home == core, chip // 4 == slot)
    sent_either(num_in, num_send, kept, SLOTS - 1)
    sent_either(stat_in, stat_send, kept, SLOTS - 1)
    own_weight.wait()
    swaps[2].wait_recv()

    pltpu.make_async_copy(att_all, att_all, att_recv.at[0]).wait()
    rows = [att_all[quarter].reshape(128, 256) for quarter in range(4)]
    for side in range(2):
        product = jnp.zeros((128, HD), jnp.float32)
        for quarter in range(4):
            product = product + jnp.dot(
                rows[quarter], w_both[side, :, quarter].reshape(256, HD), preferred_element_type=jnp.float32
            )
        part[side] = product.astype(jnp.bfloat16).reshape(4, 32, HD)

    def part_target(n):
        return chip * 2 + n % 2, core * 4 + (y + n // 2) % 4

    def part_copy(n):
        to = part_target(n)
        return pltpu.make_async_remote_copy(
            part.at[n % 2, (y + n // 2) % 4], part_in.at[y], part_send.at[0], part_recv.at[0],
            device_id=to, device_id_type=MESH,
        )

    def part_is_far(n):
        to = part_target(n)
        return jnp.logical_or(to[0] != d, to[1] != y)

    def part_start(n, carry):
        @pl.when(part_is_far(n))
        def _():
            part_copy(n).start()

        return carry

    lax.fori_loop(0, 8, part_start, 0, unroll=True)

    @pl.when(y // 4 == core)
    def _():
        pltpu.make_async_copy(part.at[core, y % 4], part_in.at[y], part_recv.at[0]).start()

    sent(num_in, att_send, CHIPS - 1)
    pltpu.make_async_copy(part_in, part_in, part_recv.at[0]).wait()
    mixed = part_in[0].astype(jnp.float32)
    for k in range(1, NY):
        mixed = mixed + part_in[k].astype(jnp.float32)
    out_ref[...] = mixed.astype(jnp.bfloat16)
    sent_either(num_in, part_send, y // 4 == core, 8)


def per_device(
    queries, new_keys, new_values, prompt_keys, prompt_values, private_keys, private_values, parents, counts, weight
):
    bf16, f32, i32 = jnp.bfloat16, jnp.float32, jnp.int32
    dma = pltpu.SemaphoreType.DMA
    anywhere = pl.BlockSpec(memory_space=pl.ANY)
    held = [
        pltpu.with_memory_space_constraint(operand, pltpu.HBM)
        for operand in (
            queries, new_keys, new_values, prompt_keys, prompt_values, private_keys, private_values, parents, counts,
            weight.reshape(QPK, 4, 32, HD),
        )
    ]
    return pl.pallas_call(
        kernel,
        out_shape=jax.ShapeDtypeStruct((32, HD), bf16),
        in_specs=[anywhere] * 10,
        out_specs=pl.BlockSpec(memory_space=pltpu.VMEM),
        scratch_shapes=[
            pltpu.VMEM((OWN_BEAMS, QPK * HD), bf16),
            pltpu.VMEM((OWN_BEAMS, HD), bf16),
            pltpu.VMEM((OWN_BEAMS, HD), bf16),
            pltpu.SMEM((OWN_BEAMS,), i32),
            pltpu.SMEM((OWN_BEAMS,), i32),
            pltpu.VMEM((32, HD), f32),
            pltpu.VMEM((32, HD), bf16),
            pltpu.VMEM((SET, 4, 32, HD), bf16),
            pltpu.VMEM((4, 32, HD), bf16),
            pltpu.VMEM((8, HD), i32),
            pltpu.VMEM((4, 8, HD), i32),
            pltpu.VMEM((SET, 2, 256, HD), bf16),
            pltpu.VMEM((SET, 2, 256, HD), bf16),
            pltpu.VMEM((SET, HD, 512), bf16),
            pltpu.VMEM((OWN_BEAMS, PRIV, HD), bf16),
            pltpu.VMEM((OWN_BEAMS, PRIV, HD), bf16),
            pltpu.VMEM((OWN_BEAMS, HD, PRIV), bf16),
            pltpu.VMEM((2, HD, HD), f32),
            pltpu.VMEM((OWN_BEAMS, PRIV, HD), f32),
            pltpu.VMEM((2, QPK, 4, 32, HD), bf16),
            pltpu.VMEM((SET + 1, HD, HD), bf16),
            pltpu.VMEM((SET + 1, 2, HD), f32),
            pltpu.VMEM((SLOTS, 32, HD), bf16),
            pltpu.VMEM((SLOTS, 2, HD), f32),
            pltpu.VMEM((16, 256), bf16),
            pltpu.VMEM((4, SET, 16, 256), bf16),
            pltpu.VMEM((2, 4, 32, HD), bf16),
            pltpu.VMEM((NY, 32, HD), bf16),
            dma((5,)), dma((2,)), dma((2,)), dma((1,)), dma((3,)), dma((3,)),
            dma((1,)), dma((SET,)), dma((1,)), dma((1,)), dma((1,)), dma((1,)),
            dma((1,)), dma((1,)), dma((1,)), dma((1,)), dma((1,)), dma((1,)), dma((1,)), dma((1,)),
        ],
        compiler_params=pltpu.CompilerParams(
            collective_id=0, has_side_effects=True, vmem_limit_bytes=32 << 20
        ),
    )(*held)


def solution(mesh):
    placed = (
        P("beam", "head"),
        P("beam", "head"),
        P("beam", "head"),
        P(None, "beam", "head"),
        P(None, "beam", "head"),
        P("beam", None, "head"),
        P("beam", None, "head"),
        P("beam"),
        P("beam"),
        P("head", "beam"),
    )
    return jax.shard_map(per_device, mesh=mesh, in_specs=placed, out_specs=P("head", "beam"), check_vma=False)
```

```python
import math

import jax
import jax.numpy as jnp
from jax import lax
from jax.experimental import pallas as pl
from jax.experimental.pallas import tpu as pltpu
from jax.sharding import PartitionSpec as P

MESH = pl.DeviceIdType.MESH
HD = 128
QPK = 8
OWN_BEAMS = 4
BLOCK_LEN = 128
PRIV = 512
NX, NZ, NY = 4, 8, 8
CHIPS = NX * NZ
SET = 8
TO_LOG2 = 1.0 / math.sqrt(HD) / math.log(2.0)
LOWEST = -3.0e38
LAST = (((1,), (1,)), ((), ()))


def kernel(
    queries, new_keys, new_values, prompt_keys, prompt_values, private_keys, private_values, parents, counts, weight,
    out_ref,
    q_in, nk_in, nv_in, par_in, cnt_in, q_rows, q_mine, q_set, q_own, par_mine, par_all,
    keys, values, values_out, values_t, pkeys, pvalues, pvalues_t, self_rows, pscores, w_all,
    num_out, stat_out, pair_num, pair_stat, num_in, stat_in, att_mine, att_all, part, part_in,
    small_sem, kv_sem, priv_sem, w_sem, pair_send, pair_recv, w_send, w_recv, hand_send, hand_recv,
    q_send, q_recv, own_send, own_recv, par_send, par_recv,
    join_send, join_recv, num_send, num_recv, stat_send, stat_recv, att_send, att_recv, part_send, part_recv,
):
    d = lax.axis_index("beam")
    y = lax.axis_index("head")
    core = d % 2
    chip = d // 2
    x = chip // NZ
    z = chip % NZ
    request = chip // 2
    home = request // SET
    slot = request % SET
    member = d % 4

    def far_first(k):
        u, t = k % NX, k // NX
        return (2 + (u + 1) // 2 * (1 - 2 * (u % 2))) % NX, (4 + (t + 1) // 2 * (1 - 2 * (t % 2))) % NZ

    def same_core(k):
        dx, dz = far_first(k)
        return (((x + dx) % NX) * NZ + (z + dz) % NZ) * 2 + core, y

    small = [
        pltpu.make_async_copy(src, dst, small_sem.at[n])
        for n, (src, dst) in enumerate(
            ((queries, q_in), (new_keys, nk_in), (new_values, nv_in), (parents, par_in), (counts, cnt_in))
        )
    ]
    for copy in small:
        copy.start()
    barrier = pltpu.get_barrier_semaphore()

    def tell(to):
        pl.semaphore_signal(barrier, inc=1, device_id=to, device_id_type=MESH)

    def tell_same(k, carry):
        tell(same_core(k))
        return carry

    def tell_other(k, carry):
        tell(((core * 16 + (chip + 8 + k) % 16) * 2 + 1 - core, y))
        return carry

    from_x = jnp.where(y % 4 // 2 == x // 2, x, (x + NX - 1 + 2 * (x % 2)) % NX)

    def tell_column(k, carry):
        to = (y + 4 + k) % NY
        row = (from_x * NZ + z) * 2 + y // 4

        @pl.when(jnp.logical_or(row != d, to != y))
        def _():
            tell((row, to))

        return carry

    lax.fori_loop(0, CHIPS - 1, tell_same, 0, unroll=True)
    lax.fori_loop(0, 16, tell_other, 0, unroll=True)
    lax.fori_loop(0, NY, tell_column, 0, unroll=True)

    @pl.when(home != core)
    def _():
        tell((chip * 2 + 1 - core, y))
        tell(((chip + 1 - 2 * (chip % 2)) * 2 + 1 - core, y))

    private = [
        pltpu.make_async_copy(private_keys, pkeys, priv_sem.at[0]),
        pltpu.make_async_copy(private_values, pvalues, priv_sem.at[1]),
    ]
    for copy in private:
        copy.start()
    mine = pl.ds(core * SET, SET)
    theirs = pl.ds((1 - core) * SET, SET)
    cached = [
        pltpu.make_async_copy(prompt_keys.at[mine], keys.at[:, 0], kv_sem.at[0]),
        pltpu.make_async_copy(prompt_values, values, kv_sem.at[1]),
    ]
    for copy in cached:
        copy.start()
    own_weight = pltpu.make_async_copy(weight, w_all.at[0, core], w_sem.at[0])
    own_weight.start()
    pair = (chip * 2 + 1 - core, y)
    swaps = [
        pltpu.make_async_remote_copy(
            src, dst, pair_send.at[n], pair_recv.at[n], device_id=pair, device_id_type=MESH
        )
        for n, (src, dst) in enumerate(
            (
                (prompt_keys.at[theirs], keys.at[:, 1]),
                (values_out, values_t.at[:, :, pl.ds(256, 256)]),
                (weight, w_all.at[0, core]),
            )
        )
    ]

    x_pair = x + 1 - 2 * (x % 2)
    x_next = (x + NX - 1 + 2 * (x % 2)) % NX
    w_copy = pltpu.make_async_remote_copy(
        weight, w_all.at[1, core], w_send.at[0], w_recv.at[0],
        device_id=((x_next * NZ + z) * 2 + core, y), device_id_type=MESH,
    )
    w_hand = pltpu.make_async_remote_copy(
        w_all.at[1, core], w_all.at[1, core], hand_send.at[0], hand_recv.at[0], device_id=pair, device_id_type=MESH
    )

    small[0].wait()
    q_wide = q_in[...].astype(jnp.float32)
    for head in range(QPK):
        q_rows[pl.ds(head * OWN_BEAMS, OWN_BEAMS), :] = q_wide[:, head * HD : (head + 1) * HD]
    q_mine[...] = q_rows[...].astype(jnp.bfloat16)
    lane = lax.broadcasted_iota(jnp.int32, (8, HD), 1)
    small[3].wait()
    row_parent = jnp.zeros((8, HD), jnp.int32)
    for beam in range(OWN_BEAMS):
        row_parent = jnp.where(lane % OWN_BEAMS == beam, par_in[beam], row_parent)
    par_mine[...] = jnp.where(lane // 32 == member, row_parent, 0)

    private[1].wait()

    def turn_private(j, carry):
        pvalues_t[j] = pvalues[j].T
        return carry

    lax.fori_loop(0, OWN_BEAMS, turn_private, 0, unroll=True)
    cached[1].wait()

    def turn_mine(i, carry):
        values_t[i, :, 0:256] = values[core * SET + i].T
        values_out[i] = values[(1 - core) * SET + i].T
        return carry

    lax.fori_loop(0, SET, turn_mine, 0, unroll=2)
    keeps = jnp.logical_and(y // 4 == core, y % 4 // 2 == x // 2)
    pl.semaphore_wait(barrier, jnp.where(home == core, 33, 63) + jnp.where(keeps, 7, 8))

    def own_copy(j):
        to = (request * 4 + j, y)
        return (
            pltpu.make_async_remote_copy(
                q_mine, q_own.at[member], own_send.at[0], own_recv.at[0], device_id=to, device_id_type=MESH
            ),
            pltpu.make_async_remote_copy(
                par_mine, par_all.at[member], par_send.at[0], par_recv.at[0], device_id=to, device_id_type=MESH
            ),
        )

    def own_start(j, carry):
        @pl.when(j != member)
        def _():
            for copy in own_copy(j):
                copy.start()

        return carry

    def sent(blocks, sem, count):
        pltpu.make_async_copy(blocks.at[pl.ds(0, count)], blocks.at[pl.ds(0, count)], sem.at[0]).wait()

    def sent_either(blocks, sem, fewer, count):
        @pl.when(fewer)
        def _():
            sent(blocks, sem, count - 1)

        @pl.when(jnp.logical_not(fewer))
        def _():
            sent(blocks, sem, count)

    lax.fori_loop(0, 4, own_start, 0, unroll=True)
    pltpu.make_async_copy(q_mine, q_own.at[member], own_recv.at[0]).start()
    pltpu.make_async_copy(par_mine, par_all.at[member], par_recv.at[0]).start()

    def nth_request(s):
        t = s // 2
        return (z // 2 + (t + 1) // 2 * (1 - 2 * (t % 2)) + 4) % 4 + 4 * (s % 2)

    def q_target(n):
        dx, dz = far_first(CHIPS - 1 - n)
        return (((x + dx) % NX) * NZ + (z + dz) % NZ) * 2 + home

    def q_copy(n):
        return pltpu.make_async_remote_copy(
            q_mine, q_set.at[slot, member], q_send.at[0], q_recv.at[slot], device_id=(q_target(n), y), device_id_type=MESH
        )

    def q_start(n, carry):
        @pl.when(q_target(n) != d)
        def _():
            q_copy(n).start()

        return carry

    lax.fori_loop(0, CHIPS, q_start, 0, unroll=True)

    @pl.when(home == core)
    def _():
        pltpu.make_async_copy(q_mine, q_set.at[slot, member], q_recv.at[slot]).start()

    for copy in swaps:
        copy.start()
    w_copy.start()

    small[1].wait()
    small[2].wait()
    small[4].wait()
    self_rows[...] = jnp.zeros_like(self_rows)
    self_rows[0, pl.ds(0, OWN_BEAMS), :] = nk_in[...].astype(jnp.float32)
    self_rows[1, pl.ds(0, OWN_BEAMS), :] = nv_in[...].astype(jnp.float32)
    self_keys = self_rows[0].astype(jnp.bfloat16)
    self_values_t = self_rows[1].T.astype(jnp.bfloat16)

    private[0].wait()
    pltpu.make_async_copy(q_own, q_own, own_recv.at[0]).wait()
    pltpu.make_async_copy(par_all, par_all, par_recv.at[0]).wait()
    q_request = q_own[...].reshape(128, HD)
    row_parent = par_all[0] + par_all[1] + par_all[2] + par_all[3]
    row_parent = row_parent[0:1, :]
    position = lax.broadcasted_iota(jnp.int32, (PRIV, HD), 0)
    at = lax.broadcasted_iota(jnp.int32, (HD, HD), 0)
    across = lax.broadcasted_iota(jnp.int32, (HD, HD), 1)
    scores = lax.dot_general(self_keys, q_request, LAST, preferred_element_type=jnp.float32) * TO_LOG2
    is_own = jnp.logical_and(across // 32 == member, across % OWN_BEAMS == at)
    self_scores = jnp.where(is_own, scores, LOWEST)

    def private_scores(j, highest):
        got = lax.dot_general(pkeys[j], q_request, LAST, preferred_element_type=jnp.float32) * TO_LOG2
        filled = jnp.where(row_parent == d * OWN_BEAMS + j, cnt_in[j] * BLOCK_LEN, 0)
        got = jnp.where(position < filled, got, LOWEST)
        pscores[j] = got
        return jnp.maximum(highest, jnp.max(got, axis=0, keepdims=True))

    highest = lax.fori_loop(
        0, OWN_BEAMS, private_scores, jnp.max(self_scores, axis=0, keepdims=True), unroll=True
    )
    weights = jnp.where(self_scores > LOWEST, jnp.exp2(self_scores - highest), 0.0)
    total = jnp.sum(weights, axis=0, keepdims=True)
    summed = jnp.dot(self_values_t, weights.astype(jnp.bfloat16), preferred_element_type=jnp.float32)

    def private_sums(j, carry):
        total, summed = carry
        got = pscores[j]
        weights = jnp.where(got > LOWEST, jnp.exp2(got - highest), 0.0)
        total = total + jnp.sum(weights, axis=0, keepdims=True)
        summed = summed + jnp.dot(pvalues_t[j], weights.astype(jnp.bfloat16), preferred_element_type=jnp.float32)
        return total, summed

    total, summed = lax.fori_loop(0, OWN_BEAMS, private_sums, (total, summed), unroll=True)
    num_out[SET] = summed.astype(jnp.bfloat16)
    stat_out[SET, 0:1, :] = highest
    stat_out[SET, 1:2, :] = total

    joins = [
        pltpu.make_async_remote_copy(
            src, dst, join_send.at[n], join_recv.at[n], device_id=pair, device_id_type=MESH
        )
        for n, (src, dst) in enumerate(((num_out.at[SET], pair_num), (stat_out.at[SET], pair_stat)))
    ]

    @pl.when(home != core)
    def _():
        for copy in joins:
            copy.start()

    def result_copies(n):
        i = nth_request(n // 4)
        quarter = (x % 2 * 2 + z % 2 + n) % 4
        rows = pl.ds(pl.multiple_of(quarter * 32, 32), 32)
        owner = (i // 4 * 2 + quarter // 2) * NZ + (2 * (i % 4) + 4 + quarter % 2) % NZ
        to = (owner * 2 + core, y)
        return (
            to[0] != d,
            (
                pltpu.make_async_remote_copy(
                    num_out.at[i, rows], num_in.at[chip], num_send.at[0], num_recv.at[0],
                    device_id=to, device_id_type=MESH,
                ),
                pltpu.make_async_remote_copy(
                    stat_out.at[i], stat_in.at[chip], stat_send.at[0], stat_recv.at[0],
                    device_id=to, device_id_type=MESH,
                ),
            ),
            (
                pltpu.make_async_copy(num_out.at[i, rows], num_in.at[chip], num_recv.at[0]),
                pltpu.make_async_copy(stat_out.at[i], stat_in.at[chip], stat_recv.at[0]),
            ),
        )

    def result_start(n):
        remote, far, near = result_copies(n)

        @pl.when(remote)
        def _():
            for copy in far:
                copy.start()

        @pl.when(jnp.logical_not(remote))
        def _():
            for copy in near:
                copy.start()

    cached[0].wait()
    for copy in swaps[:2]:
        copy.wait_recv()

    def two_requests(pair_at, carry):
        some = [nth_request(pair_at * 2), nth_request(pair_at * 2 + 1)]
        for i in some:
            pltpu.make_async_copy(q_set.at[i], q_set.at[i], q_recv.at[i]).wait()
        done = []
        for i in some:
            rows = q_set[i].reshape(128, HD)
            scores = (
                lax.dot_general(keys[i].reshape(512, HD), rows, LAST, preferred_element_type=jnp.float32) * TO_LOG2
            )
            highest = jnp.max(scores, axis=0, keepdims=True)
            weights = jnp.exp2(scores - highest)
            total = jnp.sum(weights, axis=0, keepdims=True)
            summed = jnp.dot(values_t[i], weights.astype(jnp.bfloat16), preferred_element_type=jnp.float32)
            done.append((highest, total, summed))
        for i, (highest, total, summed) in zip(some, done, strict=True):
            stat_out[i, 0:1, :] = highest
            stat_out[i, 1:2, :] = total
            num_out[i] = summed.astype(jnp.bfloat16)

            @pl.when(jnp.logical_and(home == core, i == slot))
            def _(i=i, highest=highest, total=total, summed=summed):
                for copy in joins:
                    copy.wait_recv()
                others = (
                    (stat_out[SET, 0:1, :], stat_out[SET, 1:2, :], num_out[SET]),
                    (pair_stat[0:1, :], pair_stat[1:2, :], pair_num[...]),
                )
                top = jnp.maximum(jnp.maximum(highest, others[0][0]), others[1][0])
                share = jnp.exp2(highest - top)
                total, summed = share * total, share * summed
                for other_highest, other_total, other_summed in others:
                    share = jnp.exp2(other_highest - top)
                    total = total + share * other_total
                    summed = summed + share * other_summed.astype(jnp.float32)
                stat_out[i, 0:1, :] = top
                stat_out[i, 1:2, :] = total
                num_out[i] = summed.astype(jnp.bfloat16)

        for j in range(8):
            result_start(pair_at * 8 + j)
        return carry

    lax.fori_loop(0, SET // 2, two_requests, 0, unroll=True)

    sent(q_own, own_send, 3)
    sent(par_all, par_send, 3)
    sent_either(num_in, q_send, home == core, CHIPS)
    for copy in swaps:
        copy.wait_send()

    pltpu.make_async_copy(stat_in, stat_in, stat_recv.at[0]).wait()
    stats = [stat_in[k] for k in range(CHIPS)]
    highest = stats[0][0:1, :]
    for k in range(1, CHIPS):
        highest = jnp.maximum(highest, stats[k][0:1, :])
    shares = [jnp.exp2(stats[k][0:1, :] - highest) for k in range(CHIPS)]
    total = shares[0] * stats[0][1:2, :]
    for k in range(1, CHIPS):
        total = total + shares[k] * stats[k][1:2, :]
    pltpu.make_async_copy(num_in, num_in, num_recv.at[0]).wait()
    summed = shares[0] * num_in[0].astype(jnp.float32)
    for k in range(1, CHIPS):
        summed = summed + shares[k] * num_in[k].astype(jnp.float32)
    attended = (summed / total).astype(jnp.bfloat16).astype(jnp.float32)

    head_of = lax.broadcasted_iota(jnp.int32, (32, HD), 1) // OWN_BEAMS % QPK
    spread = jnp.concatenate(
        [jnp.where(head_of == head, attended, 0.0).astype(jnp.bfloat16) for head in range(QPK)], axis=0
    )
    beam_at = lax.broadcasted_iota(jnp.int32, (16, HD), 0)
    beam_lane = lax.broadcasted_iota(jnp.int32, (16, HD), 1)
    chosen = (beam_lane // 32 * OWN_BEAMS + beam_lane % OWN_BEAMS == beam_at).astype(jnp.float32)
    att_mine[...] = lax.dot_general(
        chosen.astype(jnp.bfloat16), spread, LAST, preferred_element_type=jnp.float32
    ).astype(jnp.bfloat16)


    place = att_all.at[x % 2 * 2 + z % 2, (z // 2 + 2) % 4]

    def att_copy(k):
        to_x = jnp.where(k % 2 == 0, x_pair, x)
        to = ((to_x * NZ + (z + far_first(2 * k - 2 * (k % 2))[1]) % NZ) * 2 + core, y)
        return pltpu.make_async_remote_copy(
            att_mine, place, att_send.at[0], att_recv.at[0], device_id=to, device_id_type=MESH
        )

    def att_start(k, carry):
        att_copy(k).start()
        return carry

    lax.fori_loop(0, 2 * NZ - 1, att_start, 0, unroll=True)
    pltpu.make_async_copy(att_mine, place, att_recv.at[0]).start()

    sent(num_in, num_send, CHIPS - 1)
    sent(stat_in, stat_send, CHIPS - 1)

    @pl.when(home != core)
    def _():
        for copy in joins:
            copy.wait_send()

    own_weight.wait()
    w_copy.wait_recv()
    w_hand.start()
    swaps[2].wait_recv()

    pltpu.make_async_copy(att_all, att_all, att_recv.at[0]).wait()
    w_hand.wait_recv()
    rows = [att_all[quarter].reshape(64, 256) for quarter in range(4)]

    def project(n, carry):
        product = jnp.zeros((64, HD), jnp.float32)
        for quarter in range(4):
            product = product + jnp.dot(
                rows[quarter], w_all[n // 2, n % 2, :, quarter].reshape(256, HD), preferred_element_type=jnp.float32
            )
        part[n // 2, n % 2] = product.astype(jnp.bfloat16).reshape(2, 32, HD)
        return carry

    lax.fori_loop(0, 4, project, 0, unroll=True)

    def part_target(n):
        to_x = jnp.where(n // 4 == 0, x_next, x)
        to_y = core * 4 + x // 2 * 2 + n % 2
        return (to_x * NZ + z) * 2 + n // 2 % 2, to_y

    def part_copy(n):
        return pltpu.make_async_remote_copy(
            part.at[1 - n // 4, n // 2 % 2, n % 2], part_in.at[y], part_send.at[0], part_recv.at[0],
            device_id=part_target(n), device_id_type=MESH,
        )

    def part_is_far(n):
        to = part_target(n)
        return jnp.logical_or(to[0] != d, to[1] != y)

    def part_start(n, carry):
        @pl.when(part_is_far(n))
        def _():
            part_copy(n).start()

        return carry

    lax.fori_loop(0, 8, part_start, 0, unroll=True)

    @pl.when(keeps)
    def _():
        pltpu.make_async_copy(
            part.at[0, core, y % 2], part_in.at[y], part_recv.at[0]
        ).start()

    sent(num_in, att_send, 2 * NZ - 1)
    pltpu.make_async_copy(part_in, part_in, part_recv.at[0]).wait()
    mixed = part_in[0].astype(jnp.float32)
    for k in range(1, NY):
        mixed = mixed + part_in[k].astype(jnp.float32)
    out_ref[...] = mixed.astype(jnp.bfloat16)
    sent_either(num_in, part_send, keeps, 8)
    w_copy.wait_send()
    w_hand.wait_send()


def per_device(
    queries, new_keys, new_values, prompt_keys, prompt_values, private_keys, private_values, parents, counts, weight
):
    bf16, f32, i32 = jnp.bfloat16, jnp.float32, jnp.int32
    dma = pltpu.SemaphoreType.DMA
    anywhere = pl.BlockSpec(memory_space=pl.ANY)
    held = [
        pltpu.with_memory_space_constraint(operand, pltpu.HBM)
        for operand in (
            queries, new_keys, new_values, prompt_keys, prompt_values, private_keys, private_values, parents, counts,
            weight.reshape(QPK, 4, 32, HD),
        )
    ]
    return pl.pallas_call(
        kernel,
        out_shape=jax.ShapeDtypeStruct((32, HD), bf16),
        in_specs=[anywhere] * 10,
        out_specs=pl.BlockSpec(memory_space=pltpu.VMEM),
        scratch_shapes=[
            pltpu.VMEM((OWN_BEAMS, QPK * HD), bf16),
            pltpu.VMEM((OWN_BEAMS, HD), bf16),
            pltpu.VMEM((OWN_BEAMS, HD), bf16),
            pltpu.SMEM((OWN_BEAMS,), i32),
            pltpu.SMEM((OWN_BEAMS,), i32),
            pltpu.VMEM((32, HD), f32),
            pltpu.VMEM((32, HD), bf16),
            pltpu.VMEM((SET, 4, 32, HD), bf16),
            pltpu.VMEM((4, 32, HD), bf16),
            pltpu.VMEM((8, HD), i32),
            pltpu.VMEM((4, 8, HD), i32),
            pltpu.VMEM((SET, 2, 256, HD), bf16),
            pltpu.VMEM((2 * SET, 256, HD), bf16),
            pltpu.VMEM((SET, HD, 256), bf16),
            pltpu.VMEM((SET, HD, 512), bf16),
            pltpu.VMEM((OWN_BEAMS, PRIV, HD), bf16),
            pltpu.VMEM((OWN_BEAMS, PRIV, HD), bf16),
            pltpu.VMEM((OWN_BEAMS, HD, PRIV), bf16),
            pltpu.VMEM((2, HD, HD), f32),
            pltpu.VMEM((OWN_BEAMS, PRIV, HD), f32),
            pltpu.VMEM((2, 2, QPK, 4, 32, HD), bf16),
            pltpu.VMEM((SET + 1, HD, HD), bf16),
            pltpu.VMEM((SET + 1, 2, HD), f32),
            pltpu.VMEM((HD, HD), bf16),
            pltpu.VMEM((2, HD), f32),
            pltpu.VMEM((CHIPS, 32, HD), bf16),
            pltpu.VMEM((CHIPS, 2, HD), f32),
            pltpu.VMEM((16, 256), bf16),
            pltpu.VMEM((4, 4, 16, 256), bf16),
            pltpu.VMEM((2, 2, 2, 32, HD), bf16),
            pltpu.VMEM((NY, 32, HD), bf16),
            dma((5,)), dma((2,)), dma((2,)), dma((1,)), dma((3,)), dma((3,)), dma((1,)), dma((1,)), dma((1,)), dma((1,)),
            dma((1,)), dma((SET,)), dma((1,)), dma((1,)), dma((1,)), dma((1,)),
            dma((2,)), dma((2,)), dma((1,)), dma((1,)), dma((1,)), dma((1,)), dma((1,)), dma((1,)), dma((1,)), dma((1,)),
        ],
        compiler_params=pltpu.CompilerParams(
            collective_id=0, has_side_effects=True, vmem_limit_bytes=32 << 20
        ),
    )(*held)


def solution(mesh):
    placed = (
        P("beam", "head"),
        P("beam", "head"),
        P("beam", "head"),
        P(None, "beam", "head"),
        P(None, "beam", "head"),
        P("beam", None, "head"),
        P("beam", None, "head"),
        P("beam"),
        P("beam"),
        P("head", "beam"),
    )
    return jax.shard_map(per_device, mesh=mesh, in_specs=placed, out_specs=P("head", "beam"), check_vma=False)
```

```python
import math

import jax
import jax.numpy as jnp
from jax import lax
from jax.experimental import pallas as pl
from jax.experimental.pallas import tpu as pltpu
from jax.sharding import PartitionSpec as P

MESH = pl.DeviceIdType.MESH
HD = 128
QPK = 8
OWN_BEAMS = 4
BLOCK_LEN = 128
PRIV = 512
NX, NZ, NY = 4, 8, 8
CHIPS = NX * NZ
DIRECT = 20
SET = 8
TO_LOG2 = 1.0 / math.sqrt(HD) / math.log(2.0)
LOWEST = -3.0e38
LAST = (((1,), (1,)), ((), ()))


def kernel(
    queries, new_keys, new_values, prompt_keys, prompt_values, private_keys, private_values, parents, counts, weight,
    out_ref,
    q_in, nk_in, nv_in, par_in, cnt_in, q_rows, q_mine, q_set, q_own, par_mine, par_all,
    keys, values, values_out, values_t, pkeys, pvalues, pvalues_t, self_rows, pscores, w_all,
    private_num, num_out, stat_out, pair_num, pair_stat, num_in, stat_in, att_mine, att_all, part, part_in,
    small_sem, kv_sem, priv_sem, w_sem, pair_send, pair_recv, w_send, w_recv, hand_send, hand_recv,
    relay_send, q_send, q_recv, own_send, own_recv, par_send, par_recv,
    join_send, join_recv, num_send, num_recv, stat_send, stat_recv, att_send, att_recv, part_send, part_recv,
):
    d = lax.axis_index("beam")
    y = lax.axis_index("head")
    core = d % 2
    chip = d // 2
    x = chip // NZ
    z = chip % NZ
    request = chip // 2
    home = request // SET
    slot = request % SET
    member = d % 4

    def far_first(k):
        u, t = k % NX, k // NX
        return (2 + (u + 1) // 2 * (1 - 2 * (u % 2))) % NX, (4 + (t + 1) // 2 * (1 - 2 * (t % 2))) % NZ

    def same_core(k):
        dx, dz = far_first(k)
        return (((x + dx) % NX) * NZ + (z + dz) % NZ) * 2 + core, y

    small = [
        pltpu.make_async_copy(src, dst, small_sem.at[n])
        for n, (src, dst) in enumerate(
            ((queries, q_in), (new_keys, nk_in), (new_values, nv_in), (parents, par_in), (counts, cnt_in))
        )
    ]
    for copy in small:
        copy.start()
    barrier = pltpu.get_barrier_semaphore()

    def tell(to):
        pl.semaphore_signal(barrier, inc=1, device_id=to, device_id_type=MESH)

    def tell_same(k, carry):
        tell(same_core(k))
        return carry

    def tell_other(k, carry):
        tell(((core * 16 + (chip + 8 + k) % 16) * 2 + 1 - core, y))
        return carry

    from_x = jnp.where(y % 4 // 2 == x // 2, x, (x + NX - 1 + 2 * (x % 2)) % NX)

    def tell_column(k, carry):
        to = (y + 4 + k) % NY
        row = (from_x * NZ + z) * 2 + y // 4

        @pl.when(jnp.logical_or(row != d, to != y))
        def _():
            tell((row, to))

        return carry

    lax.fori_loop(0, CHIPS - 1, tell_same, 0, unroll=True)
    lax.fori_loop(0, 16, tell_other, 0, unroll=True)
    lax.fori_loop(0, NY, tell_column, 0, unroll=True)

    @pl.when(home != core)
    def _():
        tell((chip * 2 + 1 - core, y))
        tell(((chip + 1 - 2 * (chip % 2)) * 2 + 1 - core, y))

    private = [
        pltpu.make_async_copy(private_keys, pkeys, priv_sem.at[0]),
        pltpu.make_async_copy(private_values, pvalues, priv_sem.at[1]),
    ]
    for copy in private:
        copy.start()
    mine = pl.ds(core * SET, SET)
    theirs = pl.ds((1 - core) * SET, SET)
    cached = [
        pltpu.make_async_copy(prompt_keys.at[mine], keys.at[:, 0], kv_sem.at[0]),
        pltpu.make_async_copy(prompt_values, values, kv_sem.at[1]),
    ]
    for copy in cached:
        copy.start()
    own_weight = pltpu.make_async_copy(weight, w_all.at[0, core], w_sem.at[0])
    own_weight.start()
    pair = (chip * 2 + 1 - core, y)
    swaps = [
        pltpu.make_async_remote_copy(
            src, dst, pair_send.at[n], pair_recv.at[n], device_id=pair, device_id_type=MESH
        )
        for n, (src, dst) in enumerate(
            (
                (prompt_keys.at[theirs], keys.at[:, 1]),
                (values_out, values_t.at[:, :, pl.ds(256, 256)]),
                (weight, w_all.at[0, core]),
            )
        )
    ]

    x_pair = x + 1 - 2 * (x % 2)
    x_next = (x + NX - 1 + 2 * (x % 2)) % NX
    w_copy = pltpu.make_async_remote_copy(
        weight, w_all.at[1, core], w_send.at[0], w_recv.at[0],
        device_id=((x_next * NZ + z) * 2 + core, y), device_id_type=MESH,
    )
    w_hand = pltpu.make_async_remote_copy(
        w_all.at[1, core], w_all.at[1, core], hand_send.at[0], hand_recv.at[0], device_id=pair, device_id_type=MESH
    )

    small[0].wait()
    q_wide = q_in[...].astype(jnp.float32)
    for head in range(QPK):
        q_rows[pl.ds(head * OWN_BEAMS, OWN_BEAMS), :] = q_wide[:, head * HD : (head + 1) * HD]
    q_mine[...] = q_rows[...].astype(jnp.bfloat16)
    lane = lax.broadcasted_iota(jnp.int32, (8, HD), 1)
    small[3].wait()
    row_parent = jnp.zeros((8, HD), jnp.int32)
    for beam in range(OWN_BEAMS):
        row_parent = jnp.where(lane % OWN_BEAMS == beam, par_in[beam], row_parent)
    par_mine[...] = jnp.where(lane // 32 == member, row_parent, 0)

    private[1].wait()

    def turn_private(j, carry):
        pvalues_t[j] = pvalues[j].T
        return carry

    lax.fori_loop(0, OWN_BEAMS, turn_private, 0, unroll=True)
    cached[1].wait()

    def turn_mine(i, carry):
        values_t[i, :, 0:256] = values[core * SET + i].T
        values_out[i] = values[(1 - core) * SET + i].T
        return carry

    lax.fori_loop(0, SET, turn_mine, 0, unroll=2)
    keeps = jnp.logical_and(y // 4 == core, y % 4 // 2 == x // 2)
    pl.semaphore_wait(barrier, jnp.where(home == core, 33, 63) + jnp.where(keeps, 7, 8))

    def own_copy(j):
        to = (request * 4 + j, y)
        return (
            pltpu.make_async_remote_copy(
                q_mine, q_own.at[member], own_send.at[0], own_recv.at[0], device_id=to, device_id_type=MESH
            ),
            pltpu.make_async_remote_copy(
                par_mine, par_all.at[member], par_send.at[0], par_recv.at[0], device_id=to, device_id_type=MESH
            ),
        )

    def own_start(j, carry):
        @pl.when(j != member)
        def _():
            for copy in own_copy(j):
                copy.start()

        return carry

    def sent(blocks, sem, count):
        pltpu.make_async_copy(blocks.at[pl.ds(0, count)], blocks.at[pl.ds(0, count)], sem.at[0]).wait()

    def sent_either(blocks, sem, fewer, count):
        @pl.when(fewer)
        def _():
            sent(blocks, sem, count - 1)

        @pl.when(jnp.logical_not(fewer))
        def _():
            sent(blocks, sem, count)

    lax.fori_loop(0, 4, own_start, 0, unroll=True)
    pltpu.make_async_copy(q_mine, q_own.at[member], own_recv.at[0]).start()
    pltpu.make_async_copy(par_mine, par_all.at[member], par_recv.at[0]).start()

    def nth_request(s):
        t = s // 2
        side = (1 - 2 * (t % 2)) * (1 - 2 * (z % 2))
        return (z // 2 + (t + 1) // 2 * side + 4) % 4 + 4 * (s % 2)

    def q_target(n):
        rest = n - NZ
        near_z = (z + far_first((CHIPS - 4 - 4 * n + CHIPS * 4) % CHIPS)[1]) % NZ
        to_x = jnp.where(n < NZ, x, (x + 1 + rest % 6 // 2) % NX)
        to_z = jnp.where(n < NZ, near_z, (z // 2 * 2 + rest // 6 * 4 + rest % 2) % NZ)
        return (to_x * NZ + to_z) * 2 + home

    def q_copy(n):
        return pltpu.make_async_remote_copy(
            q_mine, q_set.at[slot, member], q_send.at[0], q_recv.at[slot], device_id=(q_target(n), y), device_id_type=MESH
        )

    def q_start(n, carry):
        @pl.when(q_target(n) != d)
        def _():
            q_copy(n).start()

        return carry

    lax.fori_loop(0, DIRECT, q_start, 0, unroll=True)

    @pl.when(home == core)
    def _():
        pltpu.make_async_copy(q_mine, q_set.at[slot, member], q_recv.at[slot]).start()

    for copy in swaps:
        copy.start()

    small[1].wait()
    small[2].wait()
    small[4].wait()
    self_rows[...] = jnp.zeros_like(self_rows)
    self_rows[0, pl.ds(0, OWN_BEAMS), :] = nk_in[...].astype(jnp.float32)
    self_rows[1, pl.ds(0, OWN_BEAMS), :] = nv_in[...].astype(jnp.float32)
    self_keys = self_rows[0].astype(jnp.bfloat16)
    self_values_t = self_rows[1].T.astype(jnp.bfloat16)

    private[0].wait()
    pltpu.make_async_copy(q_own, q_own, own_recv.at[0]).wait()
    pltpu.make_async_copy(par_all, par_all, par_recv.at[0]).wait()

    def relay(t):
        i = nth_request(2 * t + x % 2)
        pltpu.make_async_copy(q_set.at[i], q_set.at[i], q_recv.at[i]).wait()
        for dx in (2, 1, 3):
            pltpu.make_async_remote_copy(
                q_set.at[i], q_set.at[i], relay_send.at[t - 1], q_recv.at[i],
                device_id=((((x + dx) % NX) * NZ + z) * 2 + core, y), device_id_type=MESH,
            ).start()

    q_request = q_own[...].reshape(128, HD)
    row_parent = par_all[0] + par_all[1] + par_all[2] + par_all[3]
    row_parent = row_parent[0:1, :]
    position = lax.broadcasted_iota(jnp.int32, (PRIV, HD), 0)
    at = lax.broadcasted_iota(jnp.int32, (HD, HD), 0)
    across = lax.broadcasted_iota(jnp.int32, (HD, HD), 1)
    scores = lax.dot_general(self_keys, q_request, LAST, preferred_element_type=jnp.float32) * TO_LOG2
    is_own = jnp.logical_and(across // 32 == member, across % OWN_BEAMS == at)
    self_scores = jnp.where(is_own, scores, LOWEST)

    def private_scores(j, highest):
        got = lax.dot_general(pkeys[j], q_request, LAST, preferred_element_type=jnp.float32) * TO_LOG2
        filled = jnp.where(row_parent == d * OWN_BEAMS + j, cnt_in[j] * BLOCK_LEN, 0)
        got = jnp.where(position < filled, got, LOWEST)
        pscores[j] = got
        return jnp.maximum(highest, jnp.max(got, axis=0, keepdims=True))

    highest = lax.fori_loop(
        0, OWN_BEAMS, private_scores, jnp.max(self_scores, axis=0, keepdims=True), unroll=True
    )
    weights = jnp.where(self_scores > LOWEST, jnp.exp2(self_scores - highest), 0.0)
    total = jnp.sum(weights, axis=0, keepdims=True)
    summed = jnp.dot(self_values_t, weights.astype(jnp.bfloat16), preferred_element_type=jnp.float32)

    def private_sums(j, carry):
        total, summed = carry
        got = pscores[j]
        weights = jnp.where(got > LOWEST, jnp.exp2(got - highest), 0.0)
        total = total + jnp.sum(weights, axis=0, keepdims=True)
        summed = summed + jnp.dot(pvalues_t[j], weights.astype(jnp.bfloat16), preferred_element_type=jnp.float32)
        return total, summed

    total, summed = lax.fori_loop(0, OWN_BEAMS, private_sums, (total, summed), unroll=True)
    private_num[...] = summed
    stat_out[SET, 0:1, :] = highest
    stat_out[SET, 1:2, :] = total

    joins = [
        pltpu.make_async_remote_copy(
            src, dst, join_send.at[n], join_recv.at[n], device_id=pair, device_id_type=MESH
        )
        for n, (src, dst) in enumerate(((private_num, pair_num), (stat_out.at[SET], pair_stat)))
    ]

    @pl.when(home != core)
    def _():
        for copy in joins:
            copy.start()

    @pl.when(home == core)
    def _():
        relay(1)
        relay(2)

    def result_copies(n):
        i = nth_request(n // 4)
        quarter = (x % 2 * 2 + z % 2 + n) % 4
        rows = pl.ds(pl.multiple_of(quarter * 32, 32), 32)
        owner = (i // 4 * 2 + quarter // 2) * NZ + (2 * (i % 4) + 4 + quarter % 2) % NZ
        to = (owner * 2 + core, y)
        return (
            to[0] != d,
            (
                pltpu.make_async_remote_copy(
                    num_out.at[i, rows], num_in.at[chip], num_send.at[0], num_recv.at[0],
                    device_id=to, device_id_type=MESH,
                ),
                pltpu.make_async_remote_copy(
                    stat_out.at[i], stat_in.at[chip], stat_send.at[0], stat_recv.at[0],
                    device_id=to, device_id_type=MESH,
                ),
            ),
            (
                pltpu.make_async_copy(num_out.at[i, rows], num_in.at[chip], num_recv.at[0]),
                pltpu.make_async_copy(stat_out.at[i], stat_in.at[chip], stat_recv.at[0]),
            ),
        )

    def result_start(n):
        remote, far, near = result_copies(n)

        @pl.when(remote)
        def _():
            for copy in far:
                copy.start()

        @pl.when(jnp.logical_not(remote))
        def _():
            for copy in near:
                copy.start()

    cached[0].wait()
    for copy in swaps[:2]:
        copy.wait_recv()

    def two_requests(pair_at, carry):
        some = [nth_request(pair_at * 2), nth_request(pair_at * 2 + 1)]
        for side, i in enumerate(some):

            @pl.when(jnp.logical_not(jnp.logical_and(jnp.logical_and(home == core, side == x % 2), pair_at % 3 != 0)))
            def _(i=i):
                pltpu.make_async_copy(q_set.at[i], q_set.at[i], q_recv.at[i]).wait()

        done = []
        for i in some:
            rows = q_set[i].reshape(128, HD)
            scores = (
                lax.dot_general(keys[i].reshape(512, HD), rows, LAST, preferred_element_type=jnp.float32) * TO_LOG2
            )
            highest = jnp.max(scores, axis=0, keepdims=True)
            weights = jnp.exp2(scores - highest)
            total = jnp.sum(weights, axis=0, keepdims=True)
            summed = jnp.dot(values_t[i], weights.astype(jnp.bfloat16), preferred_element_type=jnp.float32)
            done.append((highest, total, summed))
        for i, (highest, total, summed) in zip(some, done, strict=True):
            stat_out[i, 0:1, :] = highest
            stat_out[i, 1:2, :] = total
            num_out[i] = summed.astype(jnp.bfloat16)

            @pl.when(jnp.logical_and(home == core, i == slot))
            def _(i=i, highest=highest, total=total, summed=summed):
                for copy in joins:
                    copy.wait_recv()
                others = (
                    (stat_out[SET, 0:1, :], stat_out[SET, 1:2, :], private_num[...]),
                    (pair_stat[0:1, :], pair_stat[1:2, :], pair_num[...]),
                )
                top = jnp.maximum(jnp.maximum(highest, others[0][0]), others[1][0])
                share = jnp.exp2(highest - top)
                total, summed = share * total, share * summed
                for other_highest, other_total, other_summed in others:
                    share = jnp.exp2(other_highest - top)
                    total = total + share * other_total
                    summed = summed + share * other_summed
                stat_out[i, 0:1, :] = top
                stat_out[i, 1:2, :] = total
                num_out[i] = summed.astype(jnp.bfloat16)

        for j in range(8):
            result_start(pair_at * 8 + j)
        return carry

    lax.fori_loop(0, SET // 2, two_requests, 0, unroll=True)
    w_copy.start()

    sent(q_own, own_send, 3)
    sent(par_all, par_send, 3)
    sent_either(num_in, q_send, home == core, DIRECT)

    @pl.when(home == core)
    def _():
        for t in range(2):
            pltpu.make_async_copy(num_in.at[pl.ds(0, 12)], num_in.at[pl.ds(0, 12)], relay_send.at[t]).wait()

    for copy in swaps:
        copy.wait_send()

    pltpu.make_async_copy(stat_in, stat_in, stat_recv.at[0]).wait()
    stats = [stat_in[k] for k in range(CHIPS)]
    highest = stats[0][0:1, :]
    for k in range(1, CHIPS):
        highest = jnp.maximum(highest, stats[k][0:1, :])
    shares = [jnp.exp2(stats[k][0:1, :] - highest) for k in range(CHIPS)]
    total = shares[0] * stats[0][1:2, :]
    for k in range(1, CHIPS):
        total = total + shares[k] * stats[k][1:2, :]
    pltpu.make_async_copy(num_in, num_in, num_recv.at[0]).wait()
    summed = shares[0] * num_in[0].astype(jnp.float32)
    for k in range(1, CHIPS):
        summed = summed + shares[k] * num_in[k].astype(jnp.float32)
    attended = (summed / total).astype(jnp.bfloat16).astype(jnp.float32)

    head_of = lax.broadcasted_iota(jnp.int32, (32, HD), 1) // OWN_BEAMS % QPK
    spread = jnp.concatenate(
        [jnp.where(head_of == head, attended, 0.0).astype(jnp.bfloat16) for head in range(QPK)], axis=0
    )
    beam_at = lax.broadcasted_iota(jnp.int32, (16, HD), 0)
    beam_lane = lax.broadcasted_iota(jnp.int32, (16, HD), 1)
    chosen = (beam_lane // 32 * OWN_BEAMS + beam_lane % OWN_BEAMS == beam_at).astype(jnp.float32)
    att_mine[...] = lax.dot_general(
        chosen.astype(jnp.bfloat16), spread, LAST, preferred_element_type=jnp.float32
    ).astype(jnp.bfloat16)


    place = att_all.at[x % 2 * 2 + z % 2, (z // 2 + 2) % 4]

    def att_copy(k):
        to_x = jnp.where(k % 2 == 0, x_pair, x)
        to = ((to_x * NZ + (z + far_first(2 * k - 2 * (k % 2))[1]) % NZ) * 2 + core, y)
        return pltpu.make_async_remote_copy(
            att_mine, place, att_send.at[0], att_recv.at[0], device_id=to, device_id_type=MESH
        )

    def att_start(k, carry):
        att_copy(k).start()
        return carry

    lax.fori_loop(0, 2 * NZ - 1, att_start, 0, unroll=True)
    pltpu.make_async_copy(att_mine, place, att_recv.at[0]).start()

    sent(num_in, num_send, CHIPS - 1)
    sent(stat_in, stat_send, CHIPS - 1)

    @pl.when(home != core)
    def _():
        for copy in joins:
            copy.wait_send()

    own_weight.wait()
    w_copy.wait_recv()
    w_hand.start()
    swaps[2].wait_recv()

    pltpu.make_async_copy(att_all, att_all, att_recv.at[0]).wait()
    w_hand.wait_recv()
    rows = [att_all[quarter].reshape(64, 256) for quarter in range(4)]

    def project(n, carry):
        product = jnp.zeros((64, HD), jnp.float32)
        for quarter in range(4):
            product = product + jnp.dot(
                rows[quarter], w_all[n // 2, n % 2, :, quarter].reshape(256, HD), preferred_element_type=jnp.float32
            )
        part[n // 2, n % 2] = product.astype(jnp.bfloat16).reshape(2, 32, HD)
        return carry

    lax.fori_loop(0, 4, project, 0, unroll=True)

    def part_target(n):
        to_x = jnp.where(n // 4 == 0, x_next, x)
        to_y = core * 4 + x // 2 * 2 + n % 2
        return (to_x * NZ + z) * 2 + n // 2 % 2, to_y

    def part_copy(n):
        return pltpu.make_async_remote_copy(
            part.at[1 - n // 4, n // 2 % 2, n % 2], part_in.at[y], part_send.at[0], part_recv.at[0],
            device_id=part_target(n), device_id_type=MESH,
        )

    def part_is_far(n):
        to = part_target(n)
        return jnp.logical_or(to[0] != d, to[1] != y)

    def part_start(n, carry):
        @pl.when(part_is_far(n))
        def _():
            part_copy(n).start()

        return carry

    lax.fori_loop(0, 8, part_start, 0, unroll=True)

    @pl.when(keeps)
    def _():
        pltpu.make_async_copy(
            part.at[0, core, y % 2], part_in.at[y], part_recv.at[0]
        ).start()

    sent(num_in, att_send, 2 * NZ - 1)
    pltpu.make_async_copy(part_in, part_in, part_recv.at[0]).wait()
    mixed = part_in[0].astype(jnp.float32)
    for k in range(1, NY):
        mixed = mixed + part_in[k].astype(jnp.float32)
    out_ref[...] = mixed.astype(jnp.bfloat16)
    sent_either(num_in, part_send, keeps, 8)
    w_copy.wait_send()
    w_hand.wait_send()


def per_device(
    queries, new_keys, new_values, prompt_keys, prompt_values, private_keys, private_values, parents, counts, weight
):
    bf16, f32, i32 = jnp.bfloat16, jnp.float32, jnp.int32
    dma = pltpu.SemaphoreType.DMA
    anywhere = pl.BlockSpec(memory_space=pl.ANY)
    held = [
        pltpu.with_memory_space_constraint(operand, pltpu.HBM)
        for operand in (
            queries, new_keys, new_values, prompt_keys, prompt_values, private_keys, private_values, parents, counts,
            weight.reshape(QPK, 4, 32, HD),
        )
    ]
    return pl.pallas_call(
        kernel,
        out_shape=jax.ShapeDtypeStruct((32, HD), bf16),
        in_specs=[anywhere] * 10,
        out_specs=pl.BlockSpec(memory_space=pltpu.VMEM),
        scratch_shapes=[
            pltpu.VMEM((OWN_BEAMS, QPK * HD), bf16),
            pltpu.VMEM((OWN_BEAMS, HD), bf16),
            pltpu.VMEM((OWN_BEAMS, HD), bf16),
            pltpu.SMEM((OWN_BEAMS,), i32),
            pltpu.SMEM((OWN_BEAMS,), i32),
            pltpu.VMEM((32, HD), f32),
            pltpu.VMEM((32, HD), bf16),
            pltpu.VMEM((SET, 4, 32, HD), bf16),
            pltpu.VMEM((4, 32, HD), bf16),
            pltpu.VMEM((8, HD), i32),
            pltpu.VMEM((4, 8, HD), i32),
            pltpu.VMEM((SET, 2, 256, HD), bf16),
            pltpu.VMEM((2 * SET, 256, HD), bf16),
            pltpu.VMEM((SET, HD, 256), bf16),
            pltpu.VMEM((SET, HD, 512), bf16),
            pltpu.VMEM((OWN_BEAMS, PRIV, HD), bf16),
            pltpu.VMEM((OWN_BEAMS, PRIV, HD), bf16),
            pltpu.VMEM((OWN_BEAMS, HD, PRIV), bf16),
            pltpu.VMEM((2, HD, HD), f32),
            pltpu.VMEM((OWN_BEAMS, PRIV, HD), f32),
            pltpu.VMEM((2, 2, QPK, 4, 32, HD), bf16),
            pltpu.VMEM((HD, HD), f32),
            pltpu.VMEM((SET, HD, HD), bf16),
            pltpu.VMEM((SET + 1, 2, HD), f32),
            pltpu.VMEM((HD, HD), f32),
            pltpu.VMEM((2, HD), f32),
            pltpu.VMEM((CHIPS, 32, HD), bf16),
            pltpu.VMEM((CHIPS, 2, HD), f32),
            pltpu.VMEM((16, 256), bf16),
            pltpu.VMEM((4, 4, 16, 256), bf16),
            pltpu.VMEM((2, 2, 2, 32, HD), bf16),
            pltpu.VMEM((NY, 32, HD), bf16),
            dma((5,)), dma((2,)), dma((2,)), dma((1,)), dma((3,)), dma((3,)), dma((1,)), dma((1,)), dma((1,)), dma((1,)),
            dma((2,)), dma((1,)), dma((SET,)), dma((1,)), dma((1,)), dma((1,)), dma((1,)),
            dma((2,)), dma((2,)), dma((1,)), dma((1,)), dma((1,)), dma((1,)), dma((1,)), dma((1,)), dma((1,)), dma((1,)),
        ],
        compiler_params=pltpu.CompilerParams(
            collective_id=0, has_side_effects=True, vmem_limit_bytes=32 << 20
        ),
    )(*held)


def solution(mesh):
    placed = (
        P("beam", "head"),
        P("beam", "head"),
        P("beam", "head"),
        P(None, "beam", "head"),
        P(None, "beam", "head"),
        P("beam", None, "head"),
        P("beam", None, "head"),
        P("beam"),
        P("beam"),
        P("head", "beam"),
    )
    return jax.shard_map(per_device, mesh=mesh, in_specs=placed, out_specs=P("head", "beam"), check_vma=False)
```

```python
import math

import jax
import jax.numpy as jnp
from jax import lax
from jax.experimental import pallas as pl
from jax.experimental.pallas import tpu as pltpu
from jax.sharding import PartitionSpec as P

MESH = pl.DeviceIdType.MESH
HD = 128
QPK = 8
OWN_BEAMS = 4
BLOCK_LEN = 128
PRIV = 512
NX, NZ, NY = 4, 8, 8
CHIPS = NX * NZ
DIRECT = 20
SET = 8
TO_LOG2 = 1.0 / math.sqrt(HD) / math.log(2.0)
LOWEST = -3.0e38
LAST = (((1,), (1,)), ((), ()))


def kernel(
    queries, new_keys, new_values, prompt_keys, prompt_values, private_keys, private_values, parents, counts, weight,
    out_ref,
    q_in, nk_in, nv_in, par_in, cnt_in, q_rows, q_mine, q_set, q_own, par_mine, par_all,
    keys, values, values_out, values_t, pkeys, pvalues, pvalues_t, self_rows, pscores, w_all,
    private_num, num_out, stat_out, pair_num, pair_stat, num_in, stat_in, att_mine, att_all, part, part_in,
    small_sem, kv_sem, priv_sem, w_sem, pair_send, pair_recv, w_send, w_recv, hand_send, hand_recv,
    relay_send, q_send, q_recv, own_send, own_recv, par_send, par_recv,
    join_send, join_recv, num_send, num_recv, stat_send, stat_recv, att_send, att_recv, part_send, part_recv,
):
    d = lax.axis_index("beam")
    y = lax.axis_index("head")
    core = d % 2
    chip = d // 2
    x = chip // NZ
    z = chip % NZ
    request = chip // 2
    home = request // SET
    slot = request % SET
    member = d % 4

    def far_first(k):
        u, t = k % NX, k // NX
        return (2 + (u + 1) // 2 * (1 - 2 * (u % 2))) % NX, (4 + (t + 1) // 2 * (1 - 2 * (t % 2))) % NZ

    def same_core(k):
        dx, dz = far_first(k)
        return (((x + dx) % NX) * NZ + (z + dz) % NZ) * 2 + core, y

    small = [
        pltpu.make_async_copy(src, dst, small_sem.at[n])
        for n, (src, dst) in enumerate(
            ((queries, q_in), (new_keys, nk_in), (new_values, nv_in), (parents, par_in), (counts, cnt_in))
        )
    ]
    for copy in small:
        copy.start()
    barrier = pltpu.get_barrier_semaphore()

    def tell(to):
        pl.semaphore_signal(barrier, inc=1, device_id=to, device_id_type=MESH)

    def tell_same(k, carry):
        tell(same_core(k))
        return carry

    def tell_other(k, carry):
        dz = far_first(k // 2 * 4)[1]
        tell((((core * 2 + k % 2) * NZ + (z + dz) % NZ) * 2 + 1 - core, y))
        return carry

    from_x = jnp.where(y % 4 // 2 == x // 2, x, (x + NX - 1 + 2 * (x % 2)) % NX)

    def tell_column(k, carry):
        to = (y + 4 + k) % NY
        row = (from_x * NZ + z) * 2 + y // 4

        @pl.when(jnp.logical_or(row != d, to != y))
        def _():
            tell((row, to))

        return carry

    lax.fori_loop(0, 16, tell_same, 0, unroll=True)
    lax.fori_loop(0, 8, tell_other, 0, unroll=True)
    lax.fori_loop(16, CHIPS - 1, tell_same, 0, unroll=True)
    lax.fori_loop(8, 16, tell_other, 0, unroll=True)
    lax.fori_loop(0, NY, tell_column, 0, unroll=True)

    @pl.when(home != core)
    def _():
        tell((chip * 2 + 1 - core, y))
        tell(((chip + 1 - 2 * (chip % 2)) * 2 + 1 - core, y))

    private = [
        pltpu.make_async_copy(private_keys, pkeys, priv_sem.at[0]),
        pltpu.make_async_copy(private_values, pvalues, priv_sem.at[1]),
    ]
    for copy in private:
        copy.start()
    mine = pl.ds(core * SET, SET)
    theirs = pl.ds((1 - core) * SET, SET)
    cached = [
        pltpu.make_async_copy(prompt_keys.at[mine], keys.at[:, 0], kv_sem.at[0]),
        pltpu.make_async_copy(prompt_values, values, kv_sem.at[1]),
    ]
    for copy in cached:
        copy.start()
    own_weight = pltpu.make_async_copy(weight, w_all.at[0, core], w_sem.at[0])
    own_weight.start()
    pair = (chip * 2 + 1 - core, y)
    swaps = [
        pltpu.make_async_remote_copy(
            src, dst, pair_send.at[n], pair_recv.at[n], device_id=pair, device_id_type=MESH
        )
        for n, (src, dst) in enumerate(
            (
                (prompt_keys.at[theirs], keys.at[:, 1]),
                (values_out, values_t.at[:, :, pl.ds(256, 256)]),
                (weight, w_all.at[0, core]),
            )
        )
    ]

    x_pair = x + 1 - 2 * (x % 2)
    x_next = (x + NX - 1 + 2 * (x % 2)) % NX
    w_copy = pltpu.make_async_remote_copy(
        weight, w_all.at[1, core], w_send.at[0], w_recv.at[0],
        device_id=((x_next * NZ + z) * 2 + core, y), device_id_type=MESH,
    )
    w_hand = pltpu.make_async_remote_copy(
        w_all.at[1, core], w_all.at[1, core], hand_send.at[0], hand_recv.at[0], device_id=pair, device_id_type=MESH
    )

    small[0].wait()
    q_wide = q_in[...].astype(jnp.float32)
    for head in range(QPK):
        q_rows[pl.ds(head * OWN_BEAMS, OWN_BEAMS), :] = q_wide[:, head * HD : (head + 1) * HD]
    q_mine[...] = q_rows[...].astype(jnp.bfloat16)
    lane = lax.broadcasted_iota(jnp.int32, (8, HD), 1)
    small[3].wait()
    row_parent = jnp.zeros((8, HD), jnp.int32)
    for beam in range(OWN_BEAMS):
        row_parent = jnp.where(lane % OWN_BEAMS == beam, par_in[beam], row_parent)
    par_mine[...] = jnp.where(lane // 32 == member, row_parent, 0)

    private[1].wait()

    def turn_private(j, carry):
        pvalues_t[j] = pvalues[j].T
        return carry

    lax.fori_loop(0, OWN_BEAMS, turn_private, 0, unroll=True)
    cached[1].wait()

    def turn_mine(i, carry):
        values_t[i, :, 0:256] = values[core * SET + i].T
        values_out[i] = values[(1 - core) * SET + i].T
        return carry

    lax.fori_loop(0, SET, turn_mine, 0, unroll=2)
    keeps = jnp.logical_and(y // 4 == core, y % 4 // 2 == x // 2)
    pl.semaphore_wait(barrier, jnp.where(home == core, 33, 63) + jnp.where(keeps, 7, 8))

    def own_copy(j):
        to = (request * 4 + j, y)
        return (
            pltpu.make_async_remote_copy(
                q_mine, q_own.at[member], own_send.at[0], own_recv.at[0], device_id=to, device_id_type=MESH
            ),
            pltpu.make_async_remote_copy(
                par_mine, par_all.at[member], par_send.at[0], par_recv.at[0], device_id=to, device_id_type=MESH
            ),
        )

    def own_start(j, carry):
        @pl.when(j != member)
        def _():
            for copy in own_copy(j):
                copy.start()

        return carry

    def sent(blocks, sem, count):
        pltpu.make_async_copy(blocks.at[pl.ds(0, count)], blocks.at[pl.ds(0, count)], sem.at[0]).wait()

    def sent_either(blocks, sem, fewer, count):
        @pl.when(fewer)
        def _():
            sent(blocks, sem, count - 1)

        @pl.when(jnp.logical_not(fewer))
        def _():
            sent(blocks, sem, count)

    lax.fori_loop(0, 4, own_start, 0, unroll=True)
    pltpu.make_async_copy(q_mine, q_own.at[member], own_recv.at[0]).start()
    pltpu.make_async_copy(par_mine, par_all.at[member], par_recv.at[0]).start()

    def nth_request(s):
        t = s // 2
        side = (1 - 2 * (t % 2)) * (1 - 2 * (z % 2))
        return (z // 2 + (t + 1) // 2 * side + 4) % 4 + 4 * (s % 2)

    def q_target(n):
        rest = n - NZ
        near_z = (z + far_first((CHIPS - 4 - 4 * n + CHIPS * 4) % CHIPS)[1]) % NZ
        to_x = jnp.where(n < NZ, x, (x + 1 + rest % 6 // 2) % NX)
        to_z = jnp.where(n < NZ, near_z, (z // 2 * 2 + rest // 6 * 4 + rest % 2) % NZ)
        return (to_x * NZ + to_z) * 2 + home

    def q_copy(n):
        return pltpu.make_async_remote_copy(
            q_mine, q_set.at[slot, member], q_send.at[0], q_recv.at[slot], device_id=(q_target(n), y), device_id_type=MESH
        )

    def q_start(n, carry):
        @pl.when(q_target(n) != d)
        def _():
            q_copy(n).start()

        return carry

    lax.fori_loop(0, DIRECT, q_start, 0, unroll=True)

    @pl.when(home == core)
    def _():
        pltpu.make_async_copy(q_mine, q_set.at[slot, member], q_recv.at[slot]).start()

    for copy in swaps:
        copy.start()

    small[1].wait()
    small[2].wait()
    small[4].wait()
    self_rows[...] = jnp.zeros_like(self_rows)
    self_rows[0, pl.ds(0, OWN_BEAMS), :] = nk_in[...].astype(jnp.float32)
    self_rows[1, pl.ds(0, OWN_BEAMS), :] = nv_in[...].astype(jnp.float32)
    self_keys = self_rows[0].astype(jnp.bfloat16)
    self_values_t = self_rows[1].T.astype(jnp.bfloat16)

    private[0].wait()
    pltpu.make_async_copy(q_own, q_own, own_recv.at[0]).wait()
    pltpu.make_async_copy(par_all, par_all, par_recv.at[0]).wait()

    def relay(t):
        i = nth_request(2 * t + x % 2)
        pltpu.make_async_copy(q_set.at[i], q_set.at[i], q_recv.at[i]).wait()
        for dx in (2, 1, 3):
            pltpu.make_async_remote_copy(
                q_set.at[i], q_set.at[i], relay_send.at[t - 1], q_recv.at[i],
                device_id=((((x + dx) % NX) * NZ + z) * 2 + core, y), device_id_type=MESH,
            ).start()

    q_request = q_own[...].reshape(128, HD)
    row_parent = par_all[0] + par_all[1] + par_all[2] + par_all[3]
    row_parent = row_parent[0:1, :]
    position = lax.broadcasted_iota(jnp.int32, (PRIV, HD), 0)
    at = lax.broadcasted_iota(jnp.int32, (HD, HD), 0)
    across = lax.broadcasted_iota(jnp.int32, (HD, HD), 1)
    scores = lax.dot_general(self_keys, q_request, LAST, preferred_element_type=jnp.float32) * TO_LOG2
    is_own = jnp.logical_and(across // 32 == member, across % OWN_BEAMS == at)
    self_scores = jnp.where(is_own, scores, LOWEST)

    def private_scores(j, highest):
        got = lax.dot_general(pkeys[j], q_request, LAST, preferred_element_type=jnp.float32) * TO_LOG2
        filled = jnp.where(row_parent == d * OWN_BEAMS + j, cnt_in[j] * BLOCK_LEN, 0)
        got = jnp.where(position < filled, got, LOWEST)
        pscores[j] = got
        return jnp.maximum(highest, jnp.max(got, axis=0, keepdims=True))

    highest = lax.fori_loop(
        0, OWN_BEAMS, private_scores, jnp.max(self_scores, axis=0, keepdims=True), unroll=True
    )
    weights = jnp.where(self_scores > LOWEST, jnp.exp2(self_scores - highest), 0.0)
    total = jnp.sum(weights, axis=0, keepdims=True)
    summed = jnp.dot(self_values_t, weights.astype(jnp.bfloat16), preferred_element_type=jnp.float32)

    def private_sums(j, carry):
        total, summed = carry
        got = pscores[j]
        weights = jnp.where(got > LOWEST, jnp.exp2(got - highest), 0.0)
        total = total + jnp.sum(weights, axis=0, keepdims=True)
        summed = summed + jnp.dot(pvalues_t[j], weights.astype(jnp.bfloat16), preferred_element_type=jnp.float32)
        return total, summed

    total, summed = lax.fori_loop(0, OWN_BEAMS, private_sums, (total, summed), unroll=True)
    private_num[...] = summed
    stat_out[SET, 0:1, :] = highest
    stat_out[SET, 1:2, :] = total

    joins = [
        pltpu.make_async_remote_copy(
            src, dst, join_send.at[n], join_recv.at[n], device_id=pair, device_id_type=MESH
        )
        for n, (src, dst) in enumerate(((private_num, pair_num), (stat_out.at[SET], pair_stat)))
    ]

    @pl.when(home != core)
    def _():
        for copy in joins:
            copy.start()

    @pl.when(home == core)
    def _():
        relay(1)
        relay(2)

    def result_copies(n):
        i = nth_request(n // 4)
        quarter = (x % 2 * 2 + z % 2 + n) % 4
        rows = pl.ds(pl.multiple_of(quarter * 32, 32), 32)
        owner = (i // 4 * 2 + quarter // 2) * NZ + (2 * (i % 4) + 4 + quarter % 2) % NZ
        to = (owner * 2 + core, y)
        return (
            to[0] != d,
            (
                pltpu.make_async_remote_copy(
                    num_out.at[i, rows], num_in.at[chip], num_send.at[0], num_recv.at[0],
                    device_id=to, device_id_type=MESH,
                ),
                pltpu.make_async_remote_copy(
                    stat_out.at[i], stat_in.at[chip], stat_send.at[0], stat_recv.at[0],
                    device_id=to, device_id_type=MESH,
                ),
            ),
            (
                pltpu.make_async_copy(num_out.at[i, rows], num_in.at[chip], num_recv.at[0]),
                pltpu.make_async_copy(stat_out.at[i], stat_in.at[chip], stat_recv.at[0]),
            ),
        )

    def result_start(n):
        remote, far, near = result_copies(n)

        @pl.when(remote)
        def _():
            for copy in far:
                copy.start()

        @pl.when(jnp.logical_not(remote))
        def _():
            for copy in near:
                copy.start()

    cached[0].wait()
    for copy in swaps[:2]:
        copy.wait_recv()

    def two_requests(pair_at, carry):
        some = [nth_request(pair_at * 2), nth_request(pair_at * 2 + 1)]
        for side, i in enumerate(some):

            @pl.when(jnp.logical_not(jnp.logical_and(jnp.logical_and(home == core, side == x % 2), pair_at % 3 != 0)))
            def _(i=i):
                pltpu.make_async_copy(q_set.at[i], q_set.at[i], q_recv.at[i]).wait()

        done = []
        for i in some:
            rows = q_set[i].reshape(128, HD)
            scores = (
                lax.dot_general(keys[i].reshape(512, HD), rows, LAST, preferred_element_type=jnp.float32) * TO_LOG2
            )
            highest = jnp.max(scores, axis=0, keepdims=True)
            weights = jnp.exp2(scores - highest)
            total = jnp.sum(weights, axis=0, keepdims=True)
            summed = jnp.dot(values_t[i], weights.astype(jnp.bfloat16), preferred_element_type=jnp.float32)
            done.append((highest, total, summed))
        for i, (highest, total, summed) in zip(some, done, strict=True):
            stat_out[i, 0:1, :] = highest
            stat_out[i, 1:2, :] = total
            num_out[i] = summed.astype(jnp.bfloat16)

            @pl.when(jnp.logical_and(home == core, i == slot))
            def _(i=i, highest=highest, total=total, summed=summed):
                for copy in joins:
                    copy.wait_recv()
                others = (
                    (stat_out[SET, 0:1, :], stat_out[SET, 1:2, :], private_num[...]),
                    (pair_stat[0:1, :], pair_stat[1:2, :], pair_num[...]),
                )
                top = jnp.maximum(jnp.maximum(highest, others[0][0]), others[1][0])
                share = jnp.exp2(highest - top)
                total, summed = share * total, share * summed
                for other_highest, other_total, other_summed in others:
                    share = jnp.exp2(other_highest - top)
                    total = total + share * other_total
                    summed = summed + share * other_summed
                stat_out[i, 0:1, :] = top
                stat_out[i, 1:2, :] = total
                num_out[i] = summed.astype(jnp.bfloat16)

        for j in range(8):
            result_start(pair_at * 8 + j)
        return carry

    lax.fori_loop(0, SET // 2, two_requests, 0, unroll=True)
    w_copy.start()

    sent(q_own, own_send, 3)
    sent(par_all, par_send, 3)
    sent_either(num_in, q_send, home == core, DIRECT)

    @pl.when(home == core)
    def _():
        for t in range(2):
            pltpu.make_async_copy(num_in.at[pl.ds(0, 12)], num_in.at[pl.ds(0, 12)], relay_send.at[t]).wait()

    for copy in swaps:
        copy.wait_send()

    pltpu.make_async_copy(stat_in, stat_in, stat_recv.at[0]).wait()
    stats = [stat_in[k] for k in range(CHIPS)]
    highest = stats[0][0:1, :]
    for k in range(1, CHIPS):
        highest = jnp.maximum(highest, stats[k][0:1, :])
    shares = [jnp.exp2(stats[k][0:1, :] - highest) for k in range(CHIPS)]
    total = shares[0] * stats[0][1:2, :]
    for k in range(1, CHIPS):
        total = total + shares[k] * stats[k][1:2, :]
    pltpu.make_async_copy(num_in, num_in, num_recv.at[0]).wait()
    summed = shares[0] * num_in[0].astype(jnp.float32)
    for k in range(1, CHIPS):
        summed = summed + shares[k] * num_in[k].astype(jnp.float32)
    attended = (summed / total).astype(jnp.bfloat16).astype(jnp.float32)

    head_of = lax.broadcasted_iota(jnp.int32, (32, HD), 1) // OWN_BEAMS % QPK
    spread = jnp.concatenate(
        [jnp.where(head_of == head, attended, 0.0).astype(jnp.bfloat16) for head in range(QPK)], axis=0
    )
    beam_at = lax.broadcasted_iota(jnp.int32, (16, HD), 0)
    beam_lane = lax.broadcasted_iota(jnp.int32, (16, HD), 1)
    chosen = (beam_lane // 32 * OWN_BEAMS + beam_lane % OWN_BEAMS == beam_at).astype(jnp.float32)
    att_mine[...] = lax.dot_general(
        chosen.astype(jnp.bfloat16), spread, LAST, preferred_element_type=jnp.float32
    ).astype(jnp.bfloat16)


    place = att_all.at[x % 2 * 2 + z % 2, (z // 2 + 2) % 4]

    def att_copy(k):
        to_x = jnp.where(k < NZ, x_pair, x)
        to = ((to_x * NZ + (z + far_first(k % NZ * 4)[1]) % NZ) * 2 + core, y)
        return pltpu.make_async_remote_copy(
            att_mine, place, att_send.at[0], att_recv.at[0], device_id=to, device_id_type=MESH
        )

    def att_start(k, carry):
        att_copy(k).start()
        return carry

    lax.fori_loop(0, 2 * NZ - 1, att_start, 0, unroll=True)
    pltpu.make_async_copy(att_mine, place, att_recv.at[0]).start()

    sent(num_in, num_send, CHIPS - 1)
    sent(stat_in, stat_send, CHIPS - 1)

    @pl.when(home != core)
    def _():
        for copy in joins:
            copy.wait_send()

    own_weight.wait()
    w_copy.wait_recv()
    w_hand.start()
    swaps[2].wait_recv()

    pltpu.make_async_copy(att_all, att_all, att_recv.at[0]).wait()
    w_hand.wait_recv()
    rows = [att_all[quarter].reshape(64, 256) for quarter in range(4)]

    def project(n, carry):
        product = jnp.zeros((64, HD), jnp.float32)
        for quarter in range(4):
            product = product + jnp.dot(
                rows[quarter], w_all[n // 2, n % 2, :, quarter].reshape(256, HD), preferred_element_type=jnp.float32
            )
        part[n // 2, n % 2] = product.astype(jnp.bfloat16).reshape(2, 32, HD)
        return carry

    lax.fori_loop(0, 4, project, 0, unroll=True)

    def part_target(n):
        to_x = jnp.where(n // 4 == 0, x_next, x)
        to_y = core * 4 + x // 2 * 2 + n % 2
        return (to_x * NZ + z) * 2 + n // 2 % 2, to_y

    def part_copy(n):
        return pltpu.make_async_remote_copy(
            part.at[1 - n // 4, n // 2 % 2, n % 2], part_in.at[y], part_send.at[0], part_recv.at[0],
            device_id=part_target(n), device_id_type=MESH,
        )

    def part_is_far(n):
        to = part_target(n)
        return jnp.logical_or(to[0] != d, to[1] != y)

    def part_start(n, carry):
        @pl.when(part_is_far(n))
        def _():
            part_copy(n).start()

        return carry

    lax.fori_loop(0, 8, part_start, 0, unroll=True)

    @pl.when(keeps)
    def _():
        pltpu.make_async_copy(
            part.at[0, core, y % 2], part_in.at[y], part_recv.at[0]
        ).start()

    sent(num_in, att_send, 2 * NZ - 1)
    pltpu.make_async_copy(part_in, part_in, part_recv.at[0]).wait()
    mixed = part_in[0].astype(jnp.float32)
    for k in range(1, NY):
        mixed = mixed + part_in[k].astype(jnp.float32)
    out_ref[...] = mixed.astype(jnp.bfloat16)
    sent_either(num_in, part_send, keeps, 8)
    w_copy.wait_send()
    w_hand.wait_send()


def per_device(
    queries, new_keys, new_values, prompt_keys, prompt_values, private_keys, private_values, parents, counts, weight
):
    bf16, f32, i32 = jnp.bfloat16, jnp.float32, jnp.int32
    dma = pltpu.SemaphoreType.DMA
    anywhere = pl.BlockSpec(memory_space=pl.ANY)
    held = [
        pltpu.with_memory_space_constraint(operand, pltpu.HBM)
        for operand in (
            queries, new_keys, new_values, prompt_keys, prompt_values, private_keys, private_values, parents, counts,
            weight.reshape(QPK, 4, 32, HD),
        )
    ]
    return pl.pallas_call(
        kernel,
        out_shape=jax.ShapeDtypeStruct((32, HD), bf16),
        in_specs=[anywhere] * 10,
        out_specs=pl.BlockSpec(memory_space=pltpu.VMEM),
        scratch_shapes=[
            pltpu.VMEM((OWN_BEAMS, QPK * HD), bf16),
            pltpu.VMEM((OWN_BEAMS, HD), bf16),
            pltpu.VMEM((OWN_BEAMS, HD), bf16),
            pltpu.SMEM((OWN_BEAMS,), i32),
            pltpu.SMEM((OWN_BEAMS,), i32),
            pltpu.VMEM((32, HD), f32),
            pltpu.VMEM((32, HD), bf16),
            pltpu.VMEM((SET, 4, 32, HD), bf16),
            pltpu.VMEM((4, 32, HD), bf16),
            pltpu.VMEM((8, HD), i32),
            pltpu.VMEM((4, 8, HD), i32),
            pltpu.VMEM((SET, 2, 256, HD), bf16),
            pltpu.VMEM((2 * SET, 256, HD), bf16),
            pltpu.VMEM((SET, HD, 256), bf16),
            pltpu.VMEM((SET, HD, 512), bf16),
            pltpu.VMEM((OWN_BEAMS, PRIV, HD), bf16),
            pltpu.VMEM((OWN_BEAMS, PRIV, HD), bf16),
            pltpu.VMEM((OWN_BEAMS, HD, PRIV), bf16),
            pltpu.VMEM((2, HD, HD), f32),
            pltpu.VMEM((OWN_BEAMS, PRIV, HD), f32),
            pltpu.VMEM((2, 2, QPK, 4, 32, HD), bf16),
            pltpu.VMEM((HD, HD), f32),
            pltpu.VMEM((SET, HD, HD), bf16),
            pltpu.VMEM((SET + 1, 2, HD), f32),
            pltpu.VMEM((HD, HD), f32),
            pltpu.VMEM((2, HD), f32),
            pltpu.VMEM((CHIPS, 32, HD), bf16),
            pltpu.VMEM((CHIPS, 2, HD), f32),
            pltpu.VMEM((16, 256), bf16),
            pltpu.VMEM((4, 4, 16, 256), bf16),
            pltpu.VMEM((2, 2, 2, 32, HD), bf16),
            pltpu.VMEM((NY, 32, HD), bf16),
            dma((5,)), dma((2,)), dma((2,)), dma((1,)), dma((3,)), dma((3,)), dma((1,)), dma((1,)), dma((1,)), dma((1,)),
            dma((2,)), dma((1,)), dma((SET,)), dma((1,)), dma((1,)), dma((1,)), dma((1,)),
            dma((2,)), dma((2,)), dma((1,)), dma((1,)), dma((1,)), dma((1,)), dma((1,)), dma((1,)), dma((1,)), dma((1,)),
        ],
        compiler_params=pltpu.CompilerParams(
            collective_id=0, has_side_effects=True, vmem_limit_bytes=32 << 20
        ),
    )(*held)


def solution(mesh):
    placed = (
        P("beam", "head"),
        P("beam", "head"),
        P("beam", "head"),
        P(None, "beam", "head"),
        P(None, "beam", "head"),
        P("beam", None, "head"),
        P("beam", None, "head"),
        P("beam"),
        P("beam"),
        P("head", "beam"),
    )
    return jax.shard_map(per_device, mesh=mesh, in_specs=placed, out_specs=P("head", "beam"), check_vma=False)
```

```python
import math

import jax
import jax.numpy as jnp
from jax import lax
from jax.experimental import pallas as pl
from jax.experimental.pallas import tpu as pltpu
from jax.sharding import PartitionSpec as P

MESH = pl.DeviceIdType.MESH
HD = 128
QPK = 8
OWN_BEAMS = 4
BLOCK_LEN = 128
PRIV = 512
NX, NZ, NY = 4, 8, 8
CHIPS = NX * NZ
DIRECT = 20
SET = 8
TO_LOG2 = 1.0 / math.sqrt(HD) / math.log(2.0)
LOWEST = -3.0e38
LAST = (((1,), (1,)), ((), ()))


def kernel(
    queries, new_keys, new_values, prompt_keys, prompt_values, private_keys, private_values, parents, counts, weight,
    out_ref,
    q_in, nk_in, nv_in, par_in, cnt_in, q_rows, q_mine, q_set, q_own, par_mine, par_all,
    keys, values, values_out, values_t, pkeys, pvalues, pvalues_t, self_rows, pscores, w_all,
    private_num, num_out, stat_out, pair_num, pair_stat, num_in, stat_in, att_mine, att_all, part, part_in,
    small_sem, kv_sem, priv_sem, w_sem, pair_send, pair_recv, w_send, w_recv, hand_send, hand_recv,
    relay_send, q_send, q_recv, own_send, own_recv, par_send, par_recv,
    join_send, join_recv, num_send, num_recv, stat_send, stat_recv, att_send, att_recv, part_send, part_recv,
):
    d = lax.axis_index("beam")
    y = lax.axis_index("head")
    core = d % 2
    chip = d // 2
    x = chip // NZ
    z = chip % NZ
    request = chip // 2
    home = request // SET
    slot = request % SET
    member = d % 4

    def far_first(k):
        u, t = k % NX, k // NX
        return (2 + (u + 1) // 2 * (1 - 2 * (u % 2))) % NX, (4 + (t + 1) // 2 * (1 - 2 * (t % 2))) % NZ

    def same_core(k):
        dx, dz = far_first(k)
        return (((x + dx) % NX) * NZ + (z + dz) % NZ) * 2 + core, y

    small = [
        pltpu.make_async_copy(src, dst, small_sem.at[n])
        for n, (src, dst) in enumerate(
            ((queries, q_in), (new_keys, nk_in), (new_values, nv_in), (parents, par_in), (counts, cnt_in))
        )
    ]
    for copy in small:
        copy.start()
    barrier = pltpu.get_barrier_semaphore()

    def tell(to):
        pl.semaphore_signal(barrier, inc=1, device_id=to, device_id_type=MESH)

    def tell_same(k, carry):
        tell(same_core(k))
        return carry

    def tell_other(k, carry):
        to_x, to_z = core * 2 + k % 2, (z + far_first(k // 2 * 4)[1]) % NZ

        @pl.when(jnp.logical_or(to_x == x, to_z // 2 % 2 == z // 2 % 2))
        def _():
            tell(((to_x * NZ + to_z) * 2 + 1 - core, y))

        return carry

    from_x = jnp.where(y % 4 // 2 == x // 2, x, (x + NX - 1 + 2 * (x % 2)) % NX)

    def tell_column(k, carry):
        to = (y + 4 + k) % NY
        row = (from_x * NZ + z) * 2 + y // 4

        @pl.when(jnp.logical_or(row != d, to != y))
        def _():
            tell((row, to))

        return carry

    lax.fori_loop(0, 16, tell_same, 0, unroll=True)
    lax.fori_loop(0, 8, tell_other, 0, unroll=True)
    lax.fori_loop(16, CHIPS - 1, tell_same, 0, unroll=True)
    lax.fori_loop(8, 16, tell_other, 0, unroll=True)
    lax.fori_loop(0, NY, tell_column, 0, unroll=True)

    @pl.when(home != core)
    def _():
        tell((chip * 2 + 1 - core, y))
        tell(((chip + 1 - 2 * (chip % 2)) * 2 + 1 - core, y))

    private = [
        pltpu.make_async_copy(private_keys, pkeys, priv_sem.at[0]),
        pltpu.make_async_copy(private_values, pvalues, priv_sem.at[1]),
    ]
    for copy in private:
        copy.start()
    mine = pl.ds(core * SET, SET)
    theirs = pl.ds((1 - core) * SET, SET)
    cached = [
        pltpu.make_async_copy(prompt_keys.at[mine], keys.at[:, 0], kv_sem.at[0]),
        pltpu.make_async_copy(prompt_values, values, kv_sem.at[1]),
    ]
    for copy in cached:
        copy.start()
    own_weight = pltpu.make_async_copy(weight, w_all.at[0, core], w_sem.at[0])
    own_weight.start()
    pair = (chip * 2 + 1 - core, y)
    swaps = [
        pltpu.make_async_remote_copy(
            src, dst, pair_send.at[n], pair_recv.at[n], device_id=pair, device_id_type=MESH
        )
        for n, (src, dst) in enumerate(
            (
                (prompt_keys.at[theirs], keys.at[:, 1]),
                (values_out, values_t.at[:, :, pl.ds(256, 256)]),
                (weight, w_all.at[0, core]),
            )
        )
    ]

    x_pair = x + 1 - 2 * (x % 2)
    x_next = (x + NX - 1 + 2 * (x % 2)) % NX
    w_copy = pltpu.make_async_remote_copy(
        weight, w_all.at[1, core], w_send.at[0], w_recv.at[0],
        device_id=((x_next * NZ + z) * 2 + core, y), device_id_type=MESH,
    )
    w_hand = pltpu.make_async_remote_copy(
        w_all.at[1, core], w_all.at[1, core], hand_send.at[0], hand_recv.at[0], device_id=pair, device_id_type=MESH
    )

    small[0].wait()
    q_wide = q_in[...].astype(jnp.float32)
    for head in range(QPK):
        q_rows[pl.ds(head * OWN_BEAMS, OWN_BEAMS), :] = q_wide[:, head * HD : (head + 1) * HD]
    q_mine[...] = q_rows[...].astype(jnp.bfloat16)
    lane = lax.broadcasted_iota(jnp.int32, (8, HD), 1)
    small[3].wait()
    row_parent = jnp.zeros((8, HD), jnp.int32)
    for beam in range(OWN_BEAMS):
        row_parent = jnp.where(lane % OWN_BEAMS == beam, par_in[beam], row_parent)
    par_mine[...] = jnp.where(lane // 32 == member, row_parent, 0)

    private[1].wait()

    def turn_private(j, carry):
        pvalues_t[j] = pvalues[j].T
        return carry

    lax.fori_loop(0, OWN_BEAMS, turn_private, 0, unroll=True)
    cached[1].wait()

    def turn_mine(i, carry):
        values_t[i, :, 0:256] = values[core * SET + i].T
        values_out[i] = values[(1 - core) * SET + i].T
        return carry

    lax.fori_loop(0, SET, turn_mine, 0, unroll=2)
    keeps = jnp.logical_and(y // 4 == core, y % 4 // 2 == x // 2)
    pl.semaphore_wait(barrier, jnp.where(home == core, 33, 51) + jnp.where(keeps, 7, 8))

    def own_copy(j):
        to = (request * 4 + j, y)
        return (
            pltpu.make_async_remote_copy(
                q_mine, q_own.at[member], own_send.at[0], own_recv.at[0], device_id=to, device_id_type=MESH
            ),
            pltpu.make_async_remote_copy(
                par_mine, par_all.at[member], par_send.at[0], par_recv.at[0], device_id=to, device_id_type=MESH
            ),
        )

    def own_start(j, carry):
        @pl.when(j != member)
        def _():
            for copy in own_copy(j):
                copy.start()

        return carry

    def sent(blocks, sem, count):
        pltpu.make_async_copy(blocks.at[pl.ds(0, count)], blocks.at[pl.ds(0, count)], sem.at[0]).wait()

    def sent_either(blocks, sem, fewer, count):
        @pl.when(fewer)
        def _():
            sent(blocks, sem, count - 1)

        @pl.when(jnp.logical_not(fewer))
        def _():
            sent(blocks, sem, count)

    lax.fori_loop(0, 4, own_start, 0, unroll=True)
    pltpu.make_async_copy(q_mine, q_own.at[member], own_recv.at[0]).start()
    pltpu.make_async_copy(par_mine, par_all.at[member], par_recv.at[0]).start()

    def nth_request(s):
        t = s // 2
        side = (1 - 2 * (t % 2)) * (1 - 2 * (z % 2))
        return (z // 2 + (t + 1) // 2 * side + 4) % 4 + 4 * (s % 2)

    def q_target(n):
        rest = n - NZ
        near_z = (z + far_first((CHIPS - 4 - 4 * n + CHIPS * 4) % CHIPS)[1]) % NZ
        to_x = jnp.where(n < NZ, x, (x + 1 + rest % 6 // 2) % NX)
        to_z = jnp.where(n < NZ, near_z, (z // 2 * 2 + rest // 6 * 4 + rest % 2) % NZ)
        return (to_x * NZ + to_z) * 2 + home

    def q_copy(n):
        return pltpu.make_async_remote_copy(
            q_mine, q_set.at[slot, member], q_send.at[0], q_recv.at[slot], device_id=(q_target(n), y), device_id_type=MESH
        )

    def q_start(n, carry):
        @pl.when(q_target(n) != d)
        def _():
            q_copy(n).start()

        return carry

    lax.fori_loop(0, DIRECT, q_start, 0, unroll=True)

    @pl.when(home == core)
    def _():
        pltpu.make_async_copy(q_mine, q_set.at[slot, member], q_recv.at[slot]).start()

    for copy in swaps:
        copy.start()

    small[1].wait()
    small[2].wait()
    small[4].wait()
    self_rows[...] = jnp.zeros_like(self_rows)
    self_rows[0, pl.ds(0, OWN_BEAMS), :] = nk_in[...].astype(jnp.float32)
    self_rows[1, pl.ds(0, OWN_BEAMS), :] = nv_in[...].astype(jnp.float32)
    self_keys = self_rows[0].astype(jnp.bfloat16)
    self_values_t = self_rows[1].T.astype(jnp.bfloat16)

    private[0].wait()
    pltpu.make_async_copy(q_own, q_own, own_recv.at[0]).wait()
    pltpu.make_async_copy(par_all, par_all, par_recv.at[0]).wait()

    def relay(t):
        i = nth_request(2 * t + x % 2)
        pltpu.make_async_copy(q_set.at[i], q_set.at[i], q_recv.at[i]).wait()
        for dx in (2, 1, 3):
            pltpu.make_async_remote_copy(
                q_set.at[i], q_set.at[i], relay_send.at[t - 1], q_recv.at[i],
                device_id=((((x + dx) % NX) * NZ + z) * 2 + core, y), device_id_type=MESH,
            ).start()

    q_request = q_own[...].reshape(128, HD)
    row_parent = par_all[0] + par_all[1] + par_all[2] + par_all[3]
    row_parent = row_parent[0:1, :]
    position = lax.broadcasted_iota(jnp.int32, (PRIV, HD), 0)
    at = lax.broadcasted_iota(jnp.int32, (HD, HD), 0)
    across = lax.broadcasted_iota(jnp.int32, (HD, HD), 1)
    scores = lax.dot_general(self_keys, q_request, LAST, preferred_element_type=jnp.float32) * TO_LOG2
    is_own = jnp.logical_and(across // 32 == member, across % OWN_BEAMS == at)
    self_scores = jnp.where(is_own, scores, LOWEST)

    def private_scores(j, highest):
        got = lax.dot_general(pkeys[j], q_request, LAST, preferred_element_type=jnp.float32) * TO_LOG2
        filled = jnp.where(row_parent == d * OWN_BEAMS + j, cnt_in[j] * BLOCK_LEN, 0)
        got = jnp.where(position < filled, got, LOWEST)
        pscores[j] = got
        return jnp.maximum(highest, jnp.max(got, axis=0, keepdims=True))

    highest = lax.fori_loop(
        0, OWN_BEAMS, private_scores, jnp.max(self_scores, axis=0, keepdims=True), unroll=True
    )
    weights = jnp.where(self_scores > LOWEST, jnp.exp2(self_scores - highest), 0.0)
    total = jnp.sum(weights, axis=0, keepdims=True)
    summed = jnp.dot(self_values_t, weights.astype(jnp.bfloat16), preferred_element_type=jnp.float32)

    def private_sums(j, carry):
        total, summed = carry
        got = pscores[j]
        weights = jnp.where(got > LOWEST, jnp.exp2(got - highest), 0.0)
        total = total + jnp.sum(weights, axis=0, keepdims=True)
        summed = summed + jnp.dot(pvalues_t[j], weights.astype(jnp.bfloat16), preferred_element_type=jnp.float32)
        return total, summed

    total, summed = lax.fori_loop(0, OWN_BEAMS, private_sums, (total, summed), unroll=True)
    private_num[...] = summed
    stat_out[SET, 0:1, :] = highest
    stat_out[SET, 1:2, :] = total

    joins = [
        pltpu.make_async_remote_copy(
            src, dst, join_send.at[n], join_recv.at[n], device_id=pair, device_id_type=MESH
        )
        for n, (src, dst) in enumerate(((private_num, pair_num), (stat_out.at[SET], pair_stat)))
    ]

    @pl.when(home != core)
    def _():
        for copy in joins:
            copy.start()

    @pl.when(home == core)
    def _():
        relay(1)
        relay(2)

    def result_copies(n):
        i = nth_request(n // 4)
        quarter = (x % 2 * 2 + z % 2 + n) % 4
        rows = pl.ds(pl.multiple_of(quarter * 32, 32), 32)
        owner = (i // 4 * 2 + quarter // 2) * NZ + (2 * (i % 4) + 4 + quarter % 2) % NZ
        to = (owner * 2 + core, y)
        return (
            to[0] != d,
            (
                pltpu.make_async_remote_copy(
                    num_out.at[i, rows], num_in.at[chip], num_send.at[0], num_recv.at[0],
                    device_id=to, device_id_type=MESH,
                ),
                pltpu.make_async_remote_copy(
                    stat_out.at[i], stat_in.at[chip], stat_send.at[0], stat_recv.at[0],
                    device_id=to, device_id_type=MESH,
                ),
            ),
            (
                pltpu.make_async_copy(num_out.at[i, rows], num_in.at[chip], num_recv.at[0]),
                pltpu.make_async_copy(stat_out.at[i], stat_in.at[chip], stat_recv.at[0]),
            ),
        )

    def result_start(n):
        remote, far, near = result_copies(n)

        @pl.when(remote)
        def _():
            for copy in far:
                copy.start()

        @pl.when(jnp.logical_not(remote))
        def _():
            for copy in near:
                copy.start()

    cached[0].wait()
    for copy in swaps[:2]:
        copy.wait_recv()

    def two_requests(pair_at, carry):
        some = [nth_request(pair_at * 2), nth_request(pair_at * 2 + 1)]
        for side, i in enumerate(some):

            @pl.when(jnp.logical_not(jnp.logical_and(jnp.logical_and(home == core, side == x % 2), pair_at % 3 != 0)))
            def _(i=i):
                pltpu.make_async_copy(q_set.at[i], q_set.at[i], q_recv.at[i]).wait()

        done = []
        for i in some:
            rows = q_set[i].reshape(128, HD)
            scores = (
                lax.dot_general(keys[i].reshape(512, HD), rows, LAST, preferred_element_type=jnp.float32) * TO_LOG2
            )
            highest = jnp.max(scores, axis=0, keepdims=True)
            weights = jnp.exp2(scores - highest)
            total = jnp.sum(weights, axis=0, keepdims=True)
            summed = jnp.dot(values_t[i], weights.astype(jnp.bfloat16), preferred_element_type=jnp.float32)
            done.append((highest, total, summed))
        for i, (highest, total, summed) in zip(some, done, strict=True):
            stat_out[i, 0:1, :] = highest
            stat_out[i, 1:2, :] = total
            num_out[i] = summed.astype(jnp.bfloat16)

            @pl.when(jnp.logical_and(home == core, i == slot))
            def _(i=i, highest=highest, total=total, summed=summed):
                for copy in joins:
                    copy.wait_recv()
                others = (
                    (stat_out[SET, 0:1, :], stat_out[SET, 1:2, :], private_num[...]),
                    (pair_stat[0:1, :], pair_stat[1:2, :], pair_num[...]),
                )
                top = jnp.maximum(jnp.maximum(highest, others[0][0]), others[1][0])
                share = jnp.exp2(highest - top)
                total, summed = share * total, share * summed
                for other_highest, other_total, other_summed in others:
                    share = jnp.exp2(other_highest - top)
                    total = total + share * other_total
                    summed = summed + share * other_summed
                stat_out[i, 0:1, :] = top
                stat_out[i, 1:2, :] = total
                num_out[i] = summed.astype(jnp.bfloat16)

        for j in range(8):
            result_start(pair_at * 8 + j)
        return carry

    lax.fori_loop(0, SET // 2, two_requests, 0, unroll=True)
    w_copy.start()

    sent(q_own, own_send, 3)
    sent(par_all, par_send, 3)
    sent_either(num_in, q_send, home == core, DIRECT)

    @pl.when(home == core)
    def _():
        for t in range(2):
            pltpu.make_async_copy(num_in.at[pl.ds(0, 12)], num_in.at[pl.ds(0, 12)], relay_send.at[t]).wait()

    for copy in swaps:
        copy.wait_send()

    pltpu.make_async_copy(stat_in, stat_in, stat_recv.at[0]).wait()
    stats = [stat_in[k] for k in range(CHIPS)]
    highest = stats[0][0:1, :]
    for k in range(1, CHIPS):
        highest = jnp.maximum(highest, stats[k][0:1, :])
    shares = [jnp.exp2(stats[k][0:1, :] - highest) for k in range(CHIPS)]
    total = shares[0] * stats[0][1:2, :]
    for k in range(1, CHIPS):
        total = total + shares[k] * stats[k][1:2, :]
    pltpu.make_async_copy(num_in, num_in, num_recv.at[0]).wait()
    summed = shares[0] * num_in[0].astype(jnp.float32)
    for k in range(1, CHIPS):
        summed = summed + shares[k] * num_in[k].astype(jnp.float32)
    attended = (summed / total).astype(jnp.bfloat16).astype(jnp.float32)

    head_of = lax.broadcasted_iota(jnp.int32, (32, HD), 1) // OWN_BEAMS % QPK
    spread = jnp.concatenate(
        [jnp.where(head_of == head, attended, 0.0).astype(jnp.bfloat16) for head in range(QPK)], axis=0
    )
    beam_at = lax.broadcasted_iota(jnp.int32, (16, HD), 0)
    beam_lane = lax.broadcasted_iota(jnp.int32, (16, HD), 1)
    chosen = (beam_lane // 32 * OWN_BEAMS + beam_lane % OWN_BEAMS == beam_at).astype(jnp.float32)
    att_mine[...] = lax.dot_general(
        chosen.astype(jnp.bfloat16), spread, LAST, preferred_element_type=jnp.float32
    ).astype(jnp.bfloat16)


    place = att_all.at[x % 2 * 2 + z % 2, (z // 2 + 2) % 4]

    def att_copy(k):
        to_x = jnp.where(k < NZ, x_pair, x)
        to = ((to_x * NZ + (z + far_first(k % NZ * 4)[1]) % NZ) * 2 + core, y)
        return pltpu.make_async_remote_copy(
            att_mine, place, att_send.at[0], att_recv.at[0], device_id=to, device_id_type=MESH
        )

    def att_start(k, carry):
        att_copy(k).start()
        return carry

    lax.fori_loop(0, 2 * NZ - 1, att_start, 0, unroll=True)
    pltpu.make_async_copy(att_mine, place, att_recv.at[0]).start()

    sent(num_in, num_send, CHIPS - 1)
    sent(stat_in, stat_send, CHIPS - 1)

    @pl.when(home != core)
    def _():
        for copy in joins:
            copy.wait_send()

    own_weight.wait()
    w_copy.wait_recv()
    w_hand.start()
    swaps[2].wait_recv()

    pltpu.make_async_copy(att_all, att_all, att_recv.at[0]).wait()
    w_hand.wait_recv()
    rows = [att_all[quarter].reshape(64, 256) for quarter in range(4)]

    def project(n, carry):
        product = jnp.zeros((64, HD), jnp.float32)
        for quarter in range(4):
            product = product + jnp.dot(
                rows[quarter], w_all[n // 2, n % 2, :, quarter].reshape(256, HD), preferred_element_type=jnp.float32
            )
        part[n // 2, n % 2] = product.astype(jnp.bfloat16).reshape(2, 32, HD)
        return carry

    lax.fori_loop(0, 4, project, 0, unroll=True)

    def part_target(n):
        to_x = jnp.where(n // 4 == 0, x_next, x)
        to_y = core * 4 + x // 2 * 2 + n % 2
        return (to_x * NZ + z) * 2 + n // 2 % 2, to_y

    def part_copy(n):
        return pltpu.make_async_remote_copy(
            part.at[1 - n // 4, n // 2 % 2, n % 2], part_in.at[y], part_send.at[0], part_recv.at[0],
            device_id=part_target(n), device_id_type=MESH,
        )

    def part_is_far(n):
        to = part_target(n)
        return jnp.logical_or(to[0] != d, to[1] != y)

    def part_start(n, carry):
        @pl.when(part_is_far(n))
        def _():
            part_copy(n).start()

        return carry

    lax.fori_loop(0, 8, part_start, 0, unroll=True)

    @pl.when(keeps)
    def _():
        pltpu.make_async_copy(
            part.at[0, core, y % 2], part_in.at[y], part_recv.at[0]
        ).start()

    sent(num_in, att_send, 2 * NZ - 1)
    pltpu.make_async_copy(part_in, part_in, part_recv.at[0]).wait()
    mixed = part_in[0].astype(jnp.float32)
    for k in range(1, NY):
        mixed = mixed + part_in[k].astype(jnp.float32)
    out_ref[...] = mixed.astype(jnp.bfloat16)
    sent_either(num_in, part_send, keeps, 8)
    w_copy.wait_send()
    w_hand.wait_send()


def per_device(
    queries, new_keys, new_values, prompt_keys, prompt_values, private_keys, private_values, parents, counts, weight
):
    bf16, f32, i32 = jnp.bfloat16, jnp.float32, jnp.int32
    dma = pltpu.SemaphoreType.DMA
    anywhere = pl.BlockSpec(memory_space=pl.ANY)
    held = [
        pltpu.with_memory_space_constraint(operand, pltpu.HBM)
        for operand in (
            queries, new_keys, new_values, prompt_keys, prompt_values, private_keys, private_values, parents, counts,
            weight.reshape(QPK, 4, 32, HD),
        )
    ]
    return pl.pallas_call(
        kernel,
        out_shape=jax.ShapeDtypeStruct((32, HD), bf16),
        in_specs=[anywhere] * 10,
        out_specs=pl.BlockSpec(memory_space=pltpu.VMEM),
        scratch_shapes=[
            pltpu.VMEM((OWN_BEAMS, QPK * HD), bf16),
            pltpu.VMEM((OWN_BEAMS, HD), bf16),
            pltpu.VMEM((OWN_BEAMS, HD), bf16),
            pltpu.SMEM((OWN_BEAMS,), i32),
            pltpu.SMEM((OWN_BEAMS,), i32),
            pltpu.VMEM((32, HD), f32),
            pltpu.VMEM((32, HD), bf16),
            pltpu.VMEM((SET, 4, 32, HD), bf16),
            pltpu.VMEM((4, 32, HD), bf16),
            pltpu.VMEM((8, HD), i32),
            pltpu.VMEM((4, 8, HD), i32),
            pltpu.VMEM((SET, 2, 256, HD), bf16),
            pltpu.VMEM((2 * SET, 256, HD), bf16),
            pltpu.VMEM((SET, HD, 256), bf16),
            pltpu.VMEM((SET, HD, 512), bf16),
            pltpu.VMEM((OWN_BEAMS, PRIV, HD), bf16),
            pltpu.VMEM((OWN_BEAMS, PRIV, HD), bf16),
            pltpu.VMEM((OWN_BEAMS, HD, PRIV), bf16),
            pltpu.VMEM((2, HD, HD), f32),
            pltpu.VMEM((OWN_BEAMS, PRIV, HD), f32),
            pltpu.VMEM((2, 2, QPK, 4, 32, HD), bf16),
            pltpu.VMEM((HD, HD), f32),
            pltpu.VMEM((SET, HD, HD), bf16),
            pltpu.VMEM((SET + 1, 2, HD), f32),
            pltpu.VMEM((HD, HD), f32),
            pltpu.VMEM((2, HD), f32),
            pltpu.VMEM((CHIPS, 32, HD), bf16),
            pltpu.VMEM((CHIPS, 2, HD), f32),
            pltpu.VMEM((16, 256), bf16),
            pltpu.VMEM((4, 4, 16, 256), bf16),
            pltpu.VMEM((2, 2, 2, 32, HD), bf16),
            pltpu.VMEM((NY, 32, HD), bf16),
            dma((5,)), dma((2,)), dma((2,)), dma((1,)), dma((3,)), dma((3,)), dma((1,)), dma((1,)), dma((1,)), dma((1,)),
            dma((2,)), dma((1,)), dma((SET,)), dma((1,)), dma((1,)), dma((1,)), dma((1,)),
            dma((2,)), dma((2,)), dma((1,)), dma((1,)), dma((1,)), dma((1,)), dma((1,)), dma((1,)), dma((1,)), dma((1,)),
        ],
        compiler_params=pltpu.CompilerParams(
            collective_id=0, has_side_effects=True, vmem_limit_bytes=32 << 20
        ),
    )(*held)


def solution(mesh):
    placed = (
        P("beam", "head"),
        P("beam", "head"),
        P("beam", "head"),
        P(None, "beam", "head"),
        P(None, "beam", "head"),
        P("beam", None, "head"),
        P("beam", None, "head"),
        P("beam"),
        P("beam"),
        P("head", "beam"),
    )
    return jax.shard_map(per_device, mesh=mesh, in_specs=placed, out_specs=P("head", "beam"), check_vma=False)
```
